256 devices in a mesh: frame: 64 (over x, z, core), head: 4 (over y).
Axes of the slice: x: 4, y: 4, z: 8, core: 2. Of those that a mesh axis runs over, the one named last changes fastest.
Arguments:
- queries: bfloat16 [16384, 1536], P(('frame', 'head')), may hold values from -40 to 40
- keys: bfloat16 [16384, 1536], P(('frame', 'head')), may hold values from -20 to 20
- values: bfloat16 [16384, 1536], P(('frame', 'head')), may hold values from -6 to 6
- band_width: int32 [64, 64], P('frame'), may hold values from 2 to 256, as said below
Outputs:
- attended: bfloat16 [16384, 1536], P(('frame', 'head'))
The draws below stay inside these ranges and needn't reach their ends.
Inputs may be any that keep to these rules, and one draw needn't show every extreme that they name: band_width[f, g] equals 256 where g == f; otherwise it lies between half of and all of 256 >> k, where k is the bit length of |f - g|.
All inputs are finite; a program needn't handle non-finite values.
Results may differ from the reference program's by a relative error of at most 0.0049.
Values may be sent and summed in bfloat16 or wider, within the bound.
No kernel may reach another device: no remote copies, remote signals or barrier semaphores. Data moves between devices by JAX's collectives and lax.ppermute only.
A program may use at most 64 MiB of HBM per device.

```python
import jax
import jax.numpy as jnp
from jax import lax

HEADS = 12
HEAD_DIM = 128
TPF = 256
BLK = 128
FRAMES = 64
TOKENS = 16384


def shared_normal(key):
    return jnp.clip(jax.random.normal(key, (TOKENS, HEADS * HEAD_DIM), jnp.float32), -4.0, 4.0)


def draw_keys(key, part):
    common = shared_normal(key)
    result = common
    return result.astype(jnp.bfloat16)


def draw_queries(key, part):
    key = jax.random.fold_in(key, 1)
    private = jnp.clip(jax.random.normal(key, (TOKENS, HEADS * HEAD_DIM), jnp.float32), -4.0, 4.0)
    result = private
    return result.astype(jnp.bfloat16)


def draw_band_width(key, part):
    key = jax.random.fold_in(key, 11)
    row_index = jnp.arange(FRAMES, dtype=jnp.int32)[:, None]
    col_index = jnp.arange(FRAMES, dtype=jnp.int32)[None, :]
    distance = jnp.abs(row_index - col_index)
    bit_level = jnp.zeros((FRAMES, FRAMES), jnp.int32)
    for exponent in range(16):
        bit_level = bit_level + (distance >= 1 << exponent).astype(jnp.int32)
    upper_band = jnp.right_shift(jnp.full((FRAMES, FRAMES), TPF, jnp.int32), bit_level)
    lower_band = upper_band // 2
    random_bits = jax.random.randint(key, (FRAMES, FRAMES), 0, 1 << 20, dtype=jnp.int32)
    band_drawn = lower_band + random_bits % (upper_band - lower_band + 1)
    band_drawn = jnp.where(random_bits // 4096 % 3 == 0, upper_band, band_drawn)
    return jnp.where(distance == 0, TPF, band_drawn).astype(jnp.int32)


def block_scale(key, dims, cuts, least, top_value):
    factor_of, own = 1.0, jax.random.fold_in(key, 6)
    for axis_at, blocks in cuts:
        heights = jnp.exp(jax.random.uniform(jax.random.fold_in(own, axis_at), (blocks,), jnp.float32, least / len(cuts), top_value / len(cuts)))
        factor_of = factor_of * jnp.repeat(heights, dims[axis_at] // blocks).reshape([-1 if axis == axis_at else 1 for axis in range(len(dims))])
    return factor_of


def centred(key, extent, scale, most, shards=(), held_as=jnp.bfloat16):
    entries = scale * jax.random.normal(key, extent, jnp.float32)
    if shards:
        entries = entries * block_scale(key, extent, shards, -0.22, 0.18)
    return jnp.clip(entries, -most, most).astype(held_as)


def setup_inputs(seed: int = 0) -> dict:
    key_list = jax.random.split(jax.random.key(seed), 5)
    return {
        "queries": draw_queries(jax.random.fold_in(key_list[4], 71), 0),
        "keys": draw_keys(jax.random.fold_in(key_list[4], 71), 0),
        "values": centred(key_list[2], (TOKENS, HEADS * HEAD_DIM), 1.0, 6.0, ((0, 256),)),
        "band_width": draw_band_width(jax.random.fold_in(key_list[4], 71), 0),
    }


def distance_list(frame_count):
    distances = [1, 2, 3]
    distance = 4
    while distance < frame_count:
        distances.append(distance)
        distance = distance * 2
    return distances


def window_of(distance, tokens, block):
    if distance == 0:
        return tokens, 0
    reach_width = tokens >> distance.bit_length()
    half_block = block // 2
    margin = -(-reach_width // half_block) * half_block
    return min(tokens, block + 2 * margin), margin


def reference(queries, keys, values, band_width):
    width = HEADS * HEAD_DIM
    query_frames = queries.reshape(FRAMES, TPF, HEADS, HEAD_DIM)
    key_frames = keys.reshape(FRAMES, TPF, HEADS, HEAD_DIM)
    value_frames = values.reshape(FRAMES, TPF, HEADS, HEAD_DIM)
    offsets = [0]
    for distance in distance_list(FRAMES):
        offsets = offsets + [-distance, distance]
    position = jnp.arange(TPF, dtype=jnp.int32)
    score_scale = HEAD_DIM ** -0.5

    def one_frame(frame):
        query_one = lax.dynamic_index_in_dim(query_frames, frame, 0, keepdims=False).astype(jnp.float32)
        prepared = []
        for offset in offsets:
            target = frame + offset
            inside = (target >= 0) & (target < FRAMES)
            clipped = jnp.clip(target, 0, FRAMES - 1).astype(jnp.int32)
            key_one = lax.dynamic_index_in_dim(key_frames, clipped, 0, keepdims=False).astype(jnp.float32)
            value_one = lax.dynamic_index_in_dim(value_frames, clipped, 0, keepdims=False).astype(jnp.float32)
            band_here = band_width[frame, clipped]
            window_len, margin = window_of(abs(offset), TPF, BLK)
            prepared.append((key_one, value_one, inside, band_here, window_len, margin))
        blocks = []
        for block_start in range(0, TPF, BLK):
            key_parts = []
            value_parts = []
            mask_parts = []
            for key_one, value_one, inside, band_here, window_len, margin in prepared:
                start = min(max(block_start - margin, 0), TPF - window_len)
                key_parts.append(key_one[start:start + window_len])
                value_parts.append(value_one[start:start + window_len])
                spacing = jnp.abs(position[block_start:block_start + BLK, None] - position[None, start:start + window_len])
                mask_parts.append(inside & (spacing <= band_here))
            key_all = jnp.concatenate(key_parts, axis=0)
            value_all = jnp.concatenate(value_parts, axis=0)
            mask_all = jnp.concatenate(mask_parts, axis=1)
            scores = jnp.einsum("qhd,khd->hqk", query_one[block_start:block_start + BLK], key_all) * score_scale
            scores = jnp.where(mask_all[None], scores, -jnp.inf)
            largest = jnp.max(scores, axis=-1, keepdims=True)
            exponent = jnp.exp(scores - largest)
            weights = (exponent / jnp.sum(exponent, axis=-1, keepdims=True)).astype(jnp.bfloat16)
            result = jnp.einsum("hqk,khd->qhd", weights.astype(jnp.float32), value_all)
            blocks.append(result.astype(jnp.bfloat16).reshape(BLK, width))
        return jnp.concatenate(blocks, axis=0)

    frames_out = lax.map(one_frame, jnp.arange(FRAMES, dtype=jnp.int32))
    return frames_out.reshape(TOKENS, width)
```

```python
import functools
import math

import jax
import jax.numpy as jnp
from jax import lax
from jax.experimental import pallas as pl
from jax.experimental.pallas import tpu as pltpu
from jax.sharding import PartitionSpec as P

HEAD_DIM = 128
TOK = 256
QUARTER = 64
HEADS_HERE = 3
W = HEADS_HERE * HEAD_DIM
XS, ZS, CS, YS = 4, 8, 2, 4
FRAMES = XS * ZS * CS
SCALE = HEAD_DIM**-0.5 * math.log2(math.e)
VMEM = pl.BlockSpec(memory_space=pltpu.VMEM)
LIGHT = pl.CostEstimate(flops=1, bytes_accessed=1, transcendentals=0)
SMEM = pl.BlockSpec(memory_space=pltpu.SMEM)


def frame_of(x, z, core):
    return ((x % XS) * ZS + z % ZS) * CS + core


def route(source):
    return [
        (frame_of(*source(x, z, c)), frame_of(x, z, c))
        for x in range(XS)
        for z in range(ZS)
        for c in range(CS)
    ]


def from_z(step):
    return route(lambda x, z, c: (x, z + step, c))


def from_x(step):
    return route(lambda x, z, c: (x + step, z, c))


def from_chip(step):
    return [((f + step * CS) % FRAMES, f) for f in range(FRAMES)]


FROM_PARTNER = route(lambda x, z, c: (x, z, 1 - c))
FROM_X_FOR_8 = route(lambda x, z, c: (x - 1 if z < ZS // 2 else x + 1, z, c))


def move(block, pairs):
    return lax.ppermute(block, "frame", pairs)


def copy_all(pairs):
    for source, out in pairs:
        out[...] = source[...]


def copier(kernel, out_shape, name):
    return lambda *arrays: pl.pallas_call(
        kernel,
        out_shape=out_shape,
        in_specs=[VMEM] * len(arrays),
        out_specs=[VMEM] * len(out_shape),
        cost_estimate=LIGHT,
        name=name,
    )(*arrays)


def bf16(rows, columns):
    return jax.ShapeDtypeStruct((rows, columns), jnp.bfloat16)


def group_at(group):
    return pl.ds(pl.multiple_of(group * W, W), W)


def quarter_at(quarter):
    return pl.ds(pl.multiple_of(quarter * QUARTER, QUARTER), QUARTER)


def pack_kernel(k_ref, v_ref, q_ref, p0, p1, p2, p3, raw_ref):
    y = lax.axis_index("head")
    pairs = []
    for step, out in enumerate((p0, p1, p2, p3)):
        for i, ref in enumerate((k_ref, v_ref, q_ref)):
            pairs.append((ref.at[:, group_at((y + step) % YS)], out.at[:, i * W : (i + 1) * W]))
    for i, ref in enumerate((k_ref, v_ref)):
        pairs.append((ref, raw_ref.at[:, i * YS * W : (i + 1) * YS * W]))
    copy_all(pairs)


def pack(keys, values, queries):
    out_shape = [bf16(QUARTER, 3 * W)] * YS + [bf16(QUARTER, 2 * YS * W)]
    return copier(pack_kernel, out_shape, "pack")(keys, values, queries)


def unpack_kernel(raw_ref, out_ref):
    pairs = []
    for g in range(YS):
        for i in range(2):
            at = (i * YS + g) * W
            out = out_ref.at[g * QUARTER : (g + 1) * QUARTER, i * W : (i + 1) * W]
            pairs.append((raw_ref.at[:, at : at + W], out))
    copy_all(pairs)


def unpack(raw):
    return copier(unpack_kernel, [bf16(TOK, 2 * W)], "unpack")(raw)[0]


def join_kernel(p0, p1, p2, p3, kv_ref, q_ref):
    y = lax.axis_index("head")
    pairs = []
    for step, piece in enumerate((p0, p1, p2, p3)):
        rows = quarter_at((y + YS - step) % YS)
        pairs.append((piece.at[:, : 2 * W], kv_ref.at[rows, :]))
        pairs.append((piece.at[:, 2 * W :], q_ref.at[rows, :]))
    copy_all(pairs)


def join(pieces):
    return copier(join_kernel, [bf16(TOK, 2 * W), bf16(TOK, W)], "join")(*pieces)


def place_kernel(p0, p1, p2, p3, out_ref):
    y = lax.axis_index("head")
    pairs = [
        (piece, out_ref.at[:, group_at((y + YS - step) % YS)])
        for step, piece in enumerate((p0, p1, p2, p3))
    ]
    copy_all(pairs)


def place(pieces):
    return copier(place_kernel, [bf16(QUARTER, YS * W)], "place")(*pieces)[0]


def y_from(step):
    return [((y - step) % YS, y) for y in range(YS)]


def over_heads(pieces):
    return [pieces[0]] + [lax.ppermute(pieces[s], "head", y_from(s)) for s in range(1, YS)]


BLOCKS = {
    "own": (lambda f, x, z, c: f, None),
    "partner": (lambda f, x, z, c: f + 1 - 2 * c, 128),
    "next1": (lambda f, x, z, c: f + 2, 64),
    "prev1": (lambda f, x, z, c: f - 2, 64),
    "next1p": (lambda f, x, z, c: f + 3 - 2 * c, 128),
    "prev1p": (lambda f, x, z, c: f - 1 - 2 * c, 128),
    "next2": (lambda f, x, z, c: f + 4, 32),
    "prev2": (lambda f, x, z, c: f - 4, 32),
    "far2p": (lambda f, x, z, c: f - 3 + 6 * c, 64),
    "z4": (lambda f, x, z, c: jnp.where(z < 4, f + 8, f - 8), 32),
    "z4x": (lambda f, x, z, c: jnp.where(z < 4, f - 8, f + 8), 32),
    "xnext": (lambda f, x, z, c: f + 16, 32),
    "xprev": (lambda f, x, z, c: f - 16, 32),
    "x2": (lambda f, x, z, c: jnp.where(x < 2, f + 32, f - 32), 32),
}
ROWS = 128
HALF = 64
FAR_STARTS = (0, 32, 96, 128)


def dot_t(a, b):
    return lax.dot_general(a, b, (((1,), (1,)), ((), ())), preferred_element_type=jnp.float32)


def attend_kernel(names, kinds, first, last, band_ref, q_ref, *refs):
    core = lax.axis_index("frame") % CS
    blocks, at = [], 0
    for kind in kinds:
        blocks.append(refs[at : at + (1 if kind == "joint" else 2)])
        at += len(blocks[-1])
    refs = refs[at:]

    def block(i, rows, columns, value):
        kind, parts = kinds[i], blocks[i]
        if kind == "split":
            return parts[value][rows, columns]
        columns = slice(columns.start + value * W, columns.stop + value * W)
        here = parts[0][rows, columns]
        if kind == "choice":
            here = jnp.where(core == 0, here, parts[1][rows, columns])
        return here

    whole = slice(0, TOK)
    if not first:
        stats_in, acc_in = refs[:2]
        refs = refs[2:]
    f = lax.axis_index("frame")
    x, z = f // (ZS * CS), (f // CS) % ZS
    bands = []
    for name in names:
        frame_at, reach = BLOCKS[name]
        if reach is None:
            bands.append(None)
            continue
        g = frame_at(f, x, z, core)
        inside = (g >= 0) & (g < FRAMES)
        bands.append(jnp.where(inside, band_ref[0, jnp.clip(g, 0, FRAMES - 1)], -1))
    far = [i for i, n in enumerate(names) if BLOCKS[n][1] == 32]
    near = [i for i in range(len(names)) if i not in far]
    gaps = {}
    for part in range(TOK // ROWS):
        row0 = part * ROWS
        gap = lax.broadcasted_iota(jnp.int32, (ROWS, TOK), 0) - lax.broadcasted_iota(
            jnp.int32, (ROWS, TOK), 1
        )
        starts = FAR_STARTS[part * 2 : part * 2 + 2]
        far_gap = lax.broadcasted_iota(jnp.int32, (HALF, ROWS), 0) - lax.broadcasted_iota(
            jnp.int32, (HALF, ROWS), 1
        )
        gaps[part] = (
            jnp.abs(gap + row0),
            jnp.abs(
                jnp.concatenate([far_gap + (row0 + j * HALF - starts[j]) for j in range(2)], axis=0)
            ),
            starts,
        )

    units = [(part, h) for part in range(TOK // ROWS) for h in range(HEADS_HERE)]
    size = len(units) if len(names) <= 2 else HEADS_HERE
    for u0 in range(0, len(units), size):
        group = units[u0 : u0 + size]
        tiles, tops, fades, ps, totals, outs = {}, {}, {}, {}, {}, {}
        for u in group:
            part, h = u
            near_gap, far_gap, starts = gaps[part]
            rows = slice(part * ROWS, (part + 1) * ROWS)
            kc = slice(h * HEAD_DIM, (h + 1) * HEAD_DIM)
            q = q_ref[rows, kc]
            for i in near:
                s = dot_t(q, block(i, whole, kc, 0)) * SCALE
                if bands[i] is not None:
                    s = jnp.where(near_gap <= bands[i], s, -jnp.inf)
                tiles[u, i] = s
            for i in far:
                s = [
                    dot_t(
                        q[j * HALF : (j + 1) * HALF],
                        block(i, slice(starts[j], starts[j] + ROWS), kc, 0),
                    )
                    for j in range(2)
                ]
                s = jnp.concatenate(s, axis=0) * SCALE
                tiles[u, i] = jnp.where(far_gap <= bands[i], s, -jnp.inf)
        for u in group:
            parts = [
                tiles[u, i][:, c0 : c0 + 128]
                for i in range(len(names))
                for c0 in range(0, tiles[u, i].shape[1], 128)
            ]
            tops[u] = jnp.max(functools.reduce(jnp.maximum, parts), axis=1, keepdims=True)
        if not first:
            for u in group:
                part, h = u
                rows = slice(part * ROWS, (part + 1) * ROWS)
                top_in = stats_in[rows, h : h + 1]
                tops[u] = jnp.maximum(tops[u], top_in)
                fades[u] = jnp.exp2(top_in - tops[u])
        for u in group:
            parts = []
            for i in range(len(names)):
                p = jnp.exp2(tiles[u, i] - tops[u])
                parts += [p[:, c0 : c0 + 128] for c0 in range(0, p.shape[1], 128)]
                ps[u, i] = p.astype(jnp.bfloat16)
            totals[u] = jnp.sum(functools.reduce(jnp.add, parts), axis=1, keepdims=True)
        for u in group:
            part, h = u
            starts = gaps[part][2]
            kc = slice(h * HEAD_DIM, (h + 1) * HEAD_DIM)
            parts = []
            for i in range(len(names)):
                p = ps[u, i]
                if i in near:
                    o = jnp.dot(p, block(i, whole, kc, 1), preferred_element_type=jnp.float32)
                else:
                    o = [
                        jnp.dot(
                            p[j * HALF : (j + 1) * HALF],
                            block(i, slice(starts[j], starts[j] + ROWS), kc, 1),
                            preferred_element_type=jnp.float32,
                        )
                        for j in range(2)
                    ]
                    o = jnp.concatenate(o, axis=0)
                parts.append(o)
            outs[u] = functools.reduce(jnp.add, parts)
        for u in group:
            part, h = u
            rows = slice(part * ROWS, (part + 1) * ROWS)
            kc = slice(h * HEAD_DIM, (h + 1) * HEAD_DIM)
            total, out = totals[u], outs[u]
            if not first:
                total = total + stats_in[rows, 4 + h : 5 + h] * fades[u]
                out = out + acc_in[rows, kc] * fades[u]
            if last:
                refs[YS][rows, kc] = (out * (1.0 / total)).astype(jnp.bfloat16)
            else:
                refs[0][rows, h : h + 1] = tops[u]
                refs[0][rows, 4 + h : 5 + h] = total
                refs[1][rows, kc] = out
    if last:
        y = lax.axis_index("head")
        for step in range(YS):
            rows = pl.ds(pl.multiple_of(((y + step) % YS) * QUARTER, QUARTER), QUARTER)
            refs[step][...] = refs[YS][rows, :]


def attend(band, q, blocks, state, last):
    names = list(blocks)
    first = state is None
    kinds, arrays = [], []
    for block in blocks.values():
        kinds.append(block[0])
        arrays += block[1:]
    if last:
        out_shape = [jax.ShapeDtypeStruct((QUARTER, W), jnp.bfloat16)] * YS
    else:
        out_shape = [
            jax.ShapeDtypeStruct((TOK, 128), jnp.float32),
            jax.ShapeDtypeStruct((TOK, W), jnp.float32),
        ]
    return pl.pallas_call(
        functools.partial(attend_kernel, names, kinds, first, last),
        out_shape=out_shape,
        in_specs=[SMEM] + [VMEM] * (1 + len(arrays) + (0 if first else 2)),
        out_specs=[VMEM] * len(out_shape),
        scratch_shapes=[pltpu.VMEM((TOK, W), jnp.bfloat16)] if last else [],
        compiler_params=pltpu.CompilerParams(vmem_limit_bytes=32 * 1024 * 1024),
        cost_estimate=LIGHT,
        name="attend" + str(len(names)),
    )(band, q, *arrays, *(() if first else state))


def shards(queries, keys, values, band):
    barrier = lax.optimization_barrier
    *pieces, raw = pack(keys, values, queries)
    z4_raw = move(raw, from_z(4))
    own, q = join(over_heads(pieces))

    xnext, xprev = move(own, from_x(1)), move(own, from_x(-1))
    next1, prev1 = move(own, from_chip(1)), move(own, from_chip(-1))
    sent, z4_raw = barrier((own, z4_raw))
    partner = move(sent, FROM_PARTNER)
    z4_packed = unpack(z4_raw)
    z4 = lax.all_to_all(z4_packed, "head", split_axis=0, concat_axis=0, tiled=True)

    def step(state, last=False, **blocks):
        blocks = {k: b if isinstance(b, tuple) else ("joint", b) for k, b in blocks.items()}
        return attend(band, q, blocks, state, last)

    state = step(None, own=own, partner=partner, xnext=xnext, xprev=xprev)

    z = (lax.axis_index("frame") // CS) % ZS
    next2 = move(jnp.where(z < 2, xnext, own), from_z(2))
    prev2 = move(jnp.where(z >= ZS - 2, xprev, own), from_z(-2))
    z4x = move(z4, FROM_X_FOR_8)
    sent, sent1, sent2, *_ = barrier((own, next1, prev1, z4))
    x2 = move(sent, from_x(2))
    next1p, prev1p = move(sent1, FROM_PARTNER), move(sent2, FROM_PARTNER)
    state = step(state, next1=next1, prev1=prev1, next1p=next1p, prev1p=prev1p, z4=z4)

    next2, prev2, state = barrier((next2, prev2, state))
    next2p, prev2p = move(next2, FROM_PARTNER), move(prev2, FROM_PARTNER)
    state = step(state, x2=x2, z4x=z4x, next2=next2, prev2=prev2)
    outs = step(state, True, far2p=("choice", prev2p, next2p))
    return place(over_heads(outs))


def solution(mesh):
    placed = (
        P(("frame", "head"), None),
        P(("frame", "head"), None),
        P(("frame", "head"), None),
        P("frame", None),
    )
    return jax.shard_map(
        shards, mesh=mesh, in_specs=placed, out_specs=P(("frame", "head"), None), check_vma=False
    )
```

```python
import functools
import math

import jax
import jax.numpy as jnp
from jax import lax
from jax.experimental import pallas as pl
from jax.experimental.pallas import tpu as pltpu
from jax.sharding import PartitionSpec as P

HEAD_DIM = 128
TOK = 256
QUARTER = 64
HEADS_HERE = 3
W = HEADS_HERE * HEAD_DIM
XS, ZS, CS, YS = 4, 8, 2, 4
FRAMES = XS * ZS * CS
SCALE = HEAD_DIM**-0.5 * math.log2(math.e)
VMEM = pl.BlockSpec(memory_space=pltpu.VMEM)
LIGHT = pl.CostEstimate(flops=1, bytes_accessed=1, transcendentals=0)
SMEM = pl.BlockSpec(memory_space=pltpu.SMEM)


def frame_of(x, z, core):
    return ((x % XS) * ZS + z % ZS) * CS + core


def route(source):
    return [
        (frame_of(*source(x, z, c)), frame_of(x, z, c))
        for x in range(XS)
        for z in range(ZS)
        for c in range(CS)
    ]


def from_z(step):
    return route(lambda x, z, c: (x, z + step, c))


def from_x(step):
    return route(lambda x, z, c: (x + step, z, c))


def from_chip(step):
    return [((f + step * CS) % FRAMES, f) for f in range(FRAMES)]


FROM_PARTNER = route(lambda x, z, c: (x, z, 1 - c))
FROM_X_FOR_8 = route(lambda x, z, c: (x - 1 if z < ZS // 2 else x + 1, z, c))


def move(block, pairs):
    return lax.ppermute(block, "frame", pairs)


def copy_all(pairs):
    for source, out in pairs:
        out[...] = source[...]


def copier(kernel, out_shape, name):
    return lambda *arrays: pl.pallas_call(
        kernel,
        out_shape=out_shape,
        in_specs=[VMEM] * len(arrays),
        out_specs=[VMEM] * len(out_shape),
        cost_estimate=LIGHT,
        name=name,
    )(*arrays)


def bf16(rows, columns):
    return jax.ShapeDtypeStruct((rows, columns), jnp.bfloat16)


def group_at(group):
    return pl.ds(pl.multiple_of(group * W, W), W)


def quarter_at(quarter):
    return pl.ds(pl.multiple_of(quarter * QUARTER, QUARTER), QUARTER)


def pack_kernel(k_ref, v_ref, q_ref, p0, p1, p2, p3, raw_ref):
    y = lax.axis_index("head")
    pairs = []
    for step, out in enumerate((p0, p1, p2, p3)):
        for i, ref in enumerate((k_ref, v_ref, q_ref)):
            pairs.append((ref.at[:, group_at((y + step) % YS)], out.at[:, i * W : (i + 1) * W]))
    for i, ref in enumerate((k_ref, v_ref)):
        pairs.append((ref, raw_ref.at[:, i * YS * W : (i + 1) * YS * W]))
    copy_all(pairs)


def pack(keys, values, queries):
    out_shape = [bf16(QUARTER, 3 * W)] * YS + [bf16(QUARTER, 2 * YS * W)]
    return copier(pack_kernel, out_shape, "pack")(keys, values, queries)


def unpack_kernel(raw_ref, out_ref):
    pairs = []
    for g in range(YS):
        for i in range(2):
            at = (i * YS + g) * W
            out = out_ref.at[g * QUARTER : (g + 1) * QUARTER, i * W : (i + 1) * W]
            pairs.append((raw_ref.at[:, at : at + W], out))
    copy_all(pairs)


def unpack(raw):
    return copier(unpack_kernel, [bf16(TOK, 2 * W)], "unpack")(raw)[0]


def join_kernel(p0, p1, p2, p3, kv_ref, q_ref):
    y = lax.axis_index("head")
    pairs = []
    for step, piece in enumerate((p0, p1, p2, p3)):
        rows = quarter_at((y + YS - step) % YS)
        pairs.append((piece.at[:, : 2 * W], kv_ref.at[rows, :]))
        pairs.append((piece.at[:, 2 * W :], q_ref.at[rows, :]))
    copy_all(pairs)


def join(pieces):
    return copier(join_kernel, [bf16(TOK, 2 * W), bf16(TOK, W)], "join")(*pieces)


def place_kernel(p0, p1, p2, p3, out_ref):
    y = lax.axis_index("head")
    pairs = [
        (piece, out_ref.at[:, group_at((y + YS - step) % YS)])
        for step, piece in enumerate((p0, p1, p2, p3))
    ]
    copy_all(pairs)


def place(pieces):
    return copier(place_kernel, [bf16(QUARTER, YS * W)], "place")(*pieces)[0]


def y_from(step):
    return [((y - step) % YS, y) for y in range(YS)]


def over_heads(pieces):
    return [pieces[0]] + [lax.ppermute(pieces[s], "head", y_from(s)) for s in range(1, YS)]


BLOCKS = {
    "own": (lambda f, x, z, c: f, None),
    "partner": (lambda f, x, z, c: f + 1 - 2 * c, 128),
    "next1": (lambda f, x, z, c: f + 2, 64),
    "prev1": (lambda f, x, z, c: f - 2, 64),
    "next1p": (lambda f, x, z, c: f + 3 - 2 * c, 128),
    "prev1p": (lambda f, x, z, c: f - 1 - 2 * c, 128),
    "next2": (lambda f, x, z, c: f + 4, 32),
    "prev2": (lambda f, x, z, c: f - 4, 32),
    "far2p": (lambda f, x, z, c: f - 3 + 6 * c, 64),
    "z4": (lambda f, x, z, c: jnp.where(z < 4, f + 8, f - 8), 32),
    "z4x": (lambda f, x, z, c: jnp.where(z < 4, f - 8, f + 8), 32),
    "xnext": (lambda f, x, z, c: f + 16, 32),
    "xprev": (lambda f, x, z, c: f - 16, 32),
    "x2": (lambda f, x, z, c: jnp.where(x < 2, f + 32, f - 32), 32),
}
ROWS = 128
HALF = 64
FAR_STARTS = (0, 32, 96, 128)


def dot_t(a, b):
    return lax.dot_general(a, b, (((1,), (1,)), ((), ())), preferred_element_type=jnp.float32)


def attend_kernel(names, kinds, first, last, band_ref, q_ref, *refs):
    core = lax.axis_index("frame") % CS
    blocks, at = [], 0
    for kind in kinds:
        blocks.append(refs[at : at + (1 if kind == "joint" else 2)])
        at += len(blocks[-1])
    refs = refs[at:]

    def block(i, rows, columns, value):
        kind, parts = kinds[i], blocks[i]
        if kind == "split":
            return parts[value][rows, columns]
        columns = slice(columns.start + value * W, columns.stop + value * W)
        here = parts[0][rows, columns]
        if kind == "choice":
            here = jnp.where(core == 0, here, parts[1][rows, columns])
        return here

    whole = slice(0, TOK)
    if not first:
        stats_in, acc_in = refs[:2]
        refs = refs[2:]
    f = lax.axis_index("frame")
    x, z = f // (ZS * CS), (f // CS) % ZS
    bands = []
    for name in names:
        frame_at, reach = BLOCKS[name]
        if reach is None:
            bands.append(None)
            continue
        g = frame_at(f, x, z, core)
        inside = (g >= 0) & (g < FRAMES)
        bands.append(jnp.where(inside, band_ref[0, jnp.clip(g, 0, FRAMES - 1)], -1))
    far = [i for i, n in enumerate(names) if BLOCKS[n][1] == 32]
    near = [i for i in range(len(names)) if i not in far]
    gaps = {}
    for part in range(TOK // ROWS):
        row0 = part * ROWS
        gap = lax.broadcasted_iota(jnp.int32, (ROWS, TOK), 0) - lax.broadcasted_iota(
            jnp.int32, (ROWS, TOK), 1
        )
        starts = FAR_STARTS[part * 2 : part * 2 + 2]
        far_gap = lax.broadcasted_iota(jnp.int32, (HALF, ROWS), 0) - lax.broadcasted_iota(
            jnp.int32, (HALF, ROWS), 1
        )
        gaps[part] = (
            jnp.abs(gap + row0),
            jnp.abs(
                jnp.concatenate([far_gap + (row0 + j * HALF - starts[j]) for j in range(2)], axis=0)
            ),
            starts,
        )

    units = [(part, h) for part in range(TOK // ROWS) for h in range(HEADS_HERE)]
    size = len(units) if len(names) <= 2 else HEADS_HERE
    for u0 in range(0, len(units), size):
        group = units[u0 : u0 + size]
        tiles, tops, fades, ps, totals, outs = {}, {}, {}, {}, {}, {}
        for u in group:
            part, h = u
            near_gap, far_gap, starts = gaps[part]
            rows = slice(part * ROWS, (part + 1) * ROWS)
            kc = slice(h * HEAD_DIM, (h + 1) * HEAD_DIM)
            q = q_ref[rows, kc]
            for i in near:
                s = dot_t(q, block(i, whole, kc, 0)) * SCALE
                if bands[i] is not None:
                    s = jnp.where(near_gap <= bands[i], s, -jnp.inf)
                tiles[u, i] = s
            for i in far:
                s = [
                    dot_t(
                        q[j * HALF : (j + 1) * HALF],
                        block(i, slice(starts[j], starts[j] + ROWS), kc, 0),
                    )
                    for j in range(2)
                ]
                s = jnp.concatenate(s, axis=0) * SCALE
                tiles[u, i] = jnp.where(far_gap <= bands[i], s, -jnp.inf)
        for u in group:
            parts = [
                tiles[u, i][:, c0 : c0 + 128]
                for i in range(len(names))
                for c0 in range(0, tiles[u, i].shape[1], 128)
            ]
            tops[u] = jnp.max(functools.reduce(jnp.maximum, parts), axis=1, keepdims=True)
        if not first:
            for u in group:
                part, h = u
                rows = slice(part * ROWS, (part + 1) * ROWS)
                top_in = stats_in[rows, h : h + 1]
                tops[u] = jnp.maximum(tops[u], top_in)
                fades[u] = jnp.exp2(top_in - tops[u])
        for u in group:
            parts = []
            for i in range(len(names)):
                p = jnp.exp2(tiles[u, i] - tops[u])
                parts += [p[:, c0 : c0 + 128] for c0 in range(0, p.shape[1], 128)]
                ps[u, i] = p.astype(jnp.bfloat16)
            totals[u] = jnp.sum(functools.reduce(jnp.add, parts), axis=1, keepdims=True)
        for u in group:
            part, h = u
            starts = gaps[part][2]
            kc = slice(h * HEAD_DIM, (h + 1) * HEAD_DIM)
            parts = []
            for i in range(len(names)):
                p = ps[u, i]
                if i in near:
                    o = jnp.dot(p, block(i, whole, kc, 1), preferred_element_type=jnp.float32)
                else:
                    o = [
                        jnp.dot(
                            p[j * HALF : (j + 1) * HALF],
                            block(i, slice(starts[j], starts[j] + ROWS), kc, 1),
                            preferred_element_type=jnp.float32,
                        )
                        for j in range(2)
                    ]
                    o = jnp.concatenate(o, axis=0)
                parts.append(o)
            outs[u] = functools.reduce(jnp.add, parts)
        for u in group:
            part, h = u
            rows = slice(part * ROWS, (part + 1) * ROWS)
            kc = slice(h * HEAD_DIM, (h + 1) * HEAD_DIM)
            total, out = totals[u], outs[u]
            if not first:
                total = total + stats_in[rows, 4 + h : 5 + h] * fades[u]
                out = out + acc_in[rows, kc] * fades[u]
            if last:
                refs[YS][rows, kc] = (out * (1.0 / total)).astype(jnp.bfloat16)
            else:
                refs[0][rows, h : h + 1] = tops[u]
                refs[0][rows, 4 + h : 5 + h] = total
                refs[1][rows, kc] = out
    if last:
        y = lax.axis_index("head")
        for step in range(YS):
            rows = pl.ds(pl.multiple_of(((y + step) % YS) * QUARTER, QUARTER), QUARTER)
            refs[step][...] = refs[YS][rows, :]


def attend(band, q, blocks, state, last):
    names = list(blocks)
    first = state is None
    kinds, arrays = [], []
    for block in blocks.values():
        kinds.append(block[0])
        arrays += block[1:]
    if last:
        out_shape = [jax.ShapeDtypeStruct((QUARTER, W), jnp.bfloat16)] * YS
    else:
        out_shape = [
            jax.ShapeDtypeStruct((TOK, 128), jnp.float32),
            jax.ShapeDtypeStruct((TOK, W), jnp.float32),
        ]
    return pl.pallas_call(
        functools.partial(attend_kernel, names, kinds, first, last),
        out_shape=out_shape,
        in_specs=[SMEM] + [VMEM] * (1 + len(arrays) + (0 if first else 2)),
        out_specs=[VMEM] * len(out_shape),
        scratch_shapes=[pltpu.VMEM((TOK, W), jnp.bfloat16)] if last else [],
        compiler_params=pltpu.CompilerParams(vmem_limit_bytes=32 * 1024 * 1024),
        cost_estimate=LIGHT,
        name="attend" + str(len(names)),
    )(band, q, *arrays, *(() if first else state))


def shards(queries, keys, values, band):
    barrier = lax.optimization_barrier
    *pieces, raw = pack(keys, values, queries)
    z4_raw = move(raw, from_z(4))
    own, q = join(over_heads(pieces))

    xnext, xprev = move(own, from_x(1)), move(own, from_x(-1))
    next1, prev1 = move(own, from_chip(1)), move(own, from_chip(-1))
    sent, z4_raw = barrier((own, z4_raw))
    partner = move(sent, FROM_PARTNER)
    z4_packed = unpack(z4_raw)
    z4 = lax.all_to_all(z4_packed, "head", split_axis=0, concat_axis=0, tiled=True)

    def step(state, last=False, **blocks):
        blocks = {k: b if isinstance(b, tuple) else ("joint", b) for k, b in blocks.items()}
        return attend(band, q, blocks, state, last)

    z = (lax.axis_index("frame") // CS) % ZS
    next2 = move(jnp.where(z < 2, xnext, own), from_z(2))
    prev2 = move(jnp.where(z >= ZS - 2, xprev, own), from_z(-2))
    z4x = move(z4, FROM_X_FOR_8)
    sent, sent1, sent2, *_ = barrier((own, next1, prev1, z4))
    x2 = move(sent, from_x(2))
    next1p, prev1p = move(sent1, FROM_PARTNER), move(sent2, FROM_PARTNER)
    next2, prev2, z4x, x2 = barrier((next2, prev2, z4x, x2))
    next2p = move(next2, FROM_PARTNER)
    sent, _ = barrier((prev2, next2p))
    prev2p = move(sent, FROM_PARTNER)
    state = step(None, own=own, xnext=xnext, xprev=xprev, z4=z4)
    state = step(
        state, partner=partner, next1=next1, prev1=prev1, next1p=next1p, prev1p=prev1p
    )
    outs = step(
        state, True, x2=x2, z4x=z4x, next2=next2, prev2=prev2, far2p=("choice", prev2p, next2p)
    )
    return place(over_heads(outs))


def solution(mesh):
    placed = (
        P(("frame", "head"), None),
        P(("frame", "head"), None),
        P(("frame", "head"), None),
        P("frame", None),
    )
    return jax.shard_map(
        shards, mesh=mesh, in_specs=placed, out_specs=P(("frame", "head"), None), check_vma=False
    )
```

```python
import functools
import math

import jax
import jax.numpy as jnp
from jax import lax
from jax.experimental import pallas as pl
from jax.experimental.pallas import tpu as pltpu
from jax.sharding import PartitionSpec as P

HEAD_DIM = 128
TOK = 256
QUARTER = 64
HEADS_HERE = 3
W = HEADS_HERE * HEAD_DIM
XS, ZS, CS, YS = 4, 8, 2, 4
FRAMES = XS * ZS * CS
SCALE = HEAD_DIM**-0.5 * math.log2(math.e)
VMEM = pl.BlockSpec(memory_space=pltpu.VMEM)
LIGHT = pl.CostEstimate(flops=1, bytes_accessed=1, transcendentals=0)
SMEM = pl.BlockSpec(memory_space=pltpu.SMEM)


def frame_of(x, z, core):
    return ((x % XS) * ZS + z % ZS) * CS + core


def route(source):
    return [
        (frame_of(*source(x, z, c)), frame_of(x, z, c))
        for x in range(XS)
        for z in range(ZS)
        for c in range(CS)
    ]


def from_z(step):
    return route(lambda x, z, c: (x, z + step, c))


def from_x(step):
    return route(lambda x, z, c: (x + step, z, c))


def from_chip(step):
    return [((f + step * CS) % FRAMES, f) for f in range(FRAMES)]


FROM_PARTNER = route(lambda x, z, c: (x, z, 1 - c))
FROM_X_FOR_8 = route(lambda x, z, c: (x - 1 if z < ZS // 2 else x + 1, z, c))


def move(block, pairs):
    return lax.ppermute(block, "frame", pairs)


def copy_all(pairs):
    for source, out in pairs:
        out[...] = source[...]


def copier(kernel, out_shape, name):
    return lambda *arrays: pl.pallas_call(
        kernel,
        out_shape=out_shape,
        in_specs=[VMEM] * len(arrays),
        out_specs=[VMEM] * len(out_shape),
        cost_estimate=LIGHT,
        name=name,
    )(*arrays)


def bf16(rows, columns):
    return jax.ShapeDtypeStruct((rows, columns), jnp.bfloat16)


def group_at(group):
    return pl.ds(pl.multiple_of(group * W, W), W)


def quarter_at(quarter):
    return pl.ds(pl.multiple_of(quarter * QUARTER, QUARTER), QUARTER)


def pack_kernel(k_ref, v_ref, q_ref, p0, p1, p2, p3, raw_ref):
    y = lax.axis_index("head")
    pairs = []
    for step, out in enumerate((p0, p1, p2, p3)):
        for i, ref in enumerate((k_ref, v_ref, q_ref)):
            pairs.append((ref.at[:, group_at((y + step) % YS)], out.at[:, i * W : (i + 1) * W]))
    for i, ref in enumerate((k_ref, v_ref)):
        pairs.append((ref, raw_ref.at[:, i * YS * W : (i + 1) * YS * W]))
    copy_all(pairs)


def pack(keys, values, queries):
    out_shape = [bf16(QUARTER, 3 * W)] * YS + [bf16(QUARTER, 2 * YS * W)]
    return copier(pack_kernel, out_shape, "pack")(keys, values, queries)


def unpack_kernel(raw_ref, out_ref):
    pairs = []
    for g in range(YS):
        for i in range(2):
            at = (i * YS + g) * W
            out = out_ref.at[g * QUARTER : (g + 1) * QUARTER, i * W : (i + 1) * W]
            pairs.append((raw_ref.at[:, at : at + W], out))
    copy_all(pairs)


def unpack(raw):
    return copier(unpack_kernel, [bf16(TOK, 2 * W)], "unpack")(raw)[0]


def join_kernel(p0, p1, p2, p3, kv_ref, q_ref):
    y = lax.axis_index("head")
    pairs = []
    for step, piece in enumerate((p0, p1, p2, p3)):
        rows = quarter_at((y + YS - step) % YS)
        pairs.append((piece.at[:, : 2 * W], kv_ref.at[rows, :]))
        pairs.append((piece.at[:, 2 * W :], q_ref.at[rows, :]))
    copy_all(pairs)


def join(pieces):
    return copier(join_kernel, [bf16(TOK, 2 * W), bf16(TOK, W)], "join")(*pieces)


def place_kernel(p0, p1, p2, p3, out_ref):
    y = lax.axis_index("head")
    pairs = [
        (piece, out_ref.at[:, group_at((y + YS - step) % YS)])
        for step, piece in enumerate((p0, p1, p2, p3))
    ]
    copy_all(pairs)


def place(pieces):
    return copier(place_kernel, [bf16(QUARTER, YS * W)], "place")(*pieces)[0]


def y_from(step):
    return [((y - step) % YS, y) for y in range(YS)]


def over_heads(pieces):
    return [pieces[0]] + [lax.ppermute(pieces[s], "head", y_from(s)) for s in range(1, YS)]


BLOCKS = {
    "own": (lambda f, x, z, c: f, None),
    "partner": (lambda f, x, z, c: f + 1 - 2 * c, 128),
    "next1": (lambda f, x, z, c: f + 2, 64),
    "prev1": (lambda f, x, z, c: f - 2, 64),
    "next1p": (lambda f, x, z, c: f + 3 - 2 * c, 128),
    "prev1p": (lambda f, x, z, c: f - 1 - 2 * c, 128),
    "next2": (lambda f, x, z, c: f + 4, 32),
    "prev2": (lambda f, x, z, c: f - 4, 32),
    "far2p": (lambda f, x, z, c: f - 3 + 6 * c, 64),
    "z4": (lambda f, x, z, c: jnp.where(z < 4, f + 8, f - 8), 32),
    "z4x": (lambda f, x, z, c: jnp.where(z < 4, f - 8, f + 8), 32),
    "xnext": (lambda f, x, z, c: f + 16, 32),
    "xprev": (lambda f, x, z, c: f - 16, 32),
    "x2": (lambda f, x, z, c: jnp.where(x < 2, f + 32, f - 32), 32),
}
ROWS = 128
HALF = 64
FAR_STARTS = (0, 32, 96, 128)


def dot_t(a, b):
    return lax.dot_general(a, b, (((1,), (1,)), ((), ())), preferred_element_type=jnp.float32)


def attend_kernel(names, kinds, first, last, band_ref, q_ref, *refs):
    core = lax.axis_index("frame") % CS
    blocks, at = [], 0
    for kind in kinds:
        blocks.append(refs[at : at + (1 if kind == "joint" else 2)])
        at += len(blocks[-1])
    refs = refs[at:]

    def block(i, rows, columns, value):
        kind, parts = kinds[i], blocks[i]
        if kind == "split":
            return parts[value][rows, columns]
        columns = slice(columns.start + value * W, columns.stop + value * W)
        here = parts[0][rows, columns]
        if kind == "choice":
            here = jnp.where(core == 0, here, parts[1][rows, columns])
        return here

    whole = slice(0, TOK)
    if not first:
        stats_in, acc_in = refs[:2]
        refs = refs[2:]
    f = lax.axis_index("frame")
    x, z = f // (ZS * CS), (f // CS) % ZS
    bands = []
    for name in names:
        frame_at, reach = BLOCKS[name]
        if reach is None:
            bands.append(None)
            continue
        g = frame_at(f, x, z, core)
        inside = (g >= 0) & (g < FRAMES)
        bands.append(jnp.where(inside, band_ref[0, jnp.clip(g, 0, FRAMES - 1)], -1))
    far = [i for i, n in enumerate(names) if BLOCKS[n][1] == 32]
    near = [i for i in range(len(names)) if i not in far]
    gaps = {}
    for part in range(TOK // ROWS):
        row0 = part * ROWS
        gap = lax.broadcasted_iota(jnp.int32, (ROWS, TOK), 0) - lax.broadcasted_iota(
            jnp.int32, (ROWS, TOK), 1
        )
        starts = FAR_STARTS[part * 2 : part * 2 + 2]
        far_gap = lax.broadcasted_iota(jnp.int32, (HALF, ROWS), 0) - lax.broadcasted_iota(
            jnp.int32, (HALF, ROWS), 1
        )
        gaps[part] = (
            jnp.abs(gap + row0),
            jnp.abs(
                jnp.concatenate([far_gap + (row0 + j * HALF - starts[j]) for j in range(2)], axis=0)
            ),
            starts,
        )

    units = [(part, h) for part in range(TOK // ROWS) for h in range(HEADS_HERE)]
    size = len(units) if len(names) <= 2 else HEADS_HERE
    for u0 in range(0, len(units), size):
        group = units[u0 : u0 + size]
        tiles, tops, fades, ps, totals, outs = {}, {}, {}, {}, {}, {}
        for u in group:
            part, h = u
            near_gap, far_gap, starts = gaps[part]
            rows = slice(part * ROWS, (part + 1) * ROWS)
            kc = slice(h * HEAD_DIM, (h + 1) * HEAD_DIM)
            q = q_ref[rows, kc]
            for i in near:
                s = dot_t(q, block(i, whole, kc, 0)) * SCALE
                if bands[i] is not None:
                    s = jnp.where(near_gap <= bands[i], s, -jnp.inf)
                tiles[u, i] = s
            for i in far:
                s = [
                    dot_t(
                        q[j * HALF : (j + 1) * HALF],
                        block(i, slice(starts[j], starts[j] + ROWS), kc, 0),
                    )
                    for j in range(2)
                ]
                s = jnp.concatenate(s, axis=0) * SCALE
                tiles[u, i] = jnp.where(far_gap <= bands[i], s, -jnp.inf)
        for u in group:
            parts = [
                tiles[u, i][:, c0 : c0 + 128]
                for i in range(len(names))
                for c0 in range(0, tiles[u, i].shape[1], 128)
            ]
            tops[u] = jnp.max(functools.reduce(jnp.maximum, parts), axis=1, keepdims=True)
        if not first:
            for u in group:
                part, h = u
                rows = slice(part * ROWS, (part + 1) * ROWS)
                top_in = stats_in[rows, h : h + 1]
                tops[u] = jnp.maximum(tops[u], top_in)
                fades[u] = jnp.exp2(top_in - tops[u])
        for u in group:
            parts = []
            for i in range(len(names)):
                p = jnp.exp2(tiles[u, i] - tops[u])
                parts += [p[:, c0 : c0 + 128] for c0 in range(0, p.shape[1], 128)]
                ps[u, i] = p.astype(jnp.bfloat16)
            totals[u] = jnp.sum(functools.reduce(jnp.add, parts), axis=1, keepdims=True)
        for u in group:
            part, h = u
            starts = gaps[part][2]
            kc = slice(h * HEAD_DIM, (h + 1) * HEAD_DIM)
            parts = []
            for i in range(len(names)):
                p = ps[u, i]
                if i in near:
                    o = jnp.dot(p, block(i, whole, kc, 1), preferred_element_type=jnp.float32)
                else:
                    o = [
                        jnp.dot(
                            p[j * HALF : (j + 1) * HALF],
                            block(i, slice(starts[j], starts[j] + ROWS), kc, 1),
                            preferred_element_type=jnp.float32,
                        )
                        for j in range(2)
                    ]
                    o = jnp.concatenate(o, axis=0)
                parts.append(o)
            outs[u] = functools.reduce(jnp.add, parts)
        for u in group:
            part, h = u
            rows = slice(part * ROWS, (part + 1) * ROWS)
            kc = slice(h * HEAD_DIM, (h + 1) * HEAD_DIM)
            total, out = totals[u], outs[u]
            if not first:
                total = total + stats_in[rows, 4 + h : 5 + h] * fades[u]
                out = out + acc_in[rows, kc] * fades[u]
            if last:
                refs[YS][rows, kc] = (out * (1.0 / total)).astype(jnp.bfloat16)
            else:
                refs[0][rows, h : h + 1] = tops[u]
                refs[0][rows, 4 + h : 5 + h] = total
                refs[1][rows, kc] = out
    if last:
        y = lax.axis_index("head")
        for step in range(YS):
            rows = pl.ds(pl.multiple_of(((y + step) % YS) * QUARTER, QUARTER), QUARTER)
            refs[step][...] = refs[YS][rows, :]


def attend(band, q, blocks, state, last):
    names = list(blocks)
    first = state is None
    kinds, arrays = [], []
    for block in blocks.values():
        kinds.append(block[0])
        arrays += block[1:]
    if last:
        out_shape = [jax.ShapeDtypeStruct((QUARTER, W), jnp.bfloat16)] * YS
    else:
        out_shape = [
            jax.ShapeDtypeStruct((TOK, 128), jnp.float32),
            jax.ShapeDtypeStruct((TOK, W), jnp.float32),
        ]
    return pl.pallas_call(
        functools.partial(attend_kernel, names, kinds, first, last),
        out_shape=out_shape,
        in_specs=[SMEM] + [VMEM] * (1 + len(arrays) + (0 if first else 2)),
        out_specs=[VMEM] * len(out_shape),
        scratch_shapes=[pltpu.VMEM((TOK, W), jnp.bfloat16)] if last else [],
        compiler_params=pltpu.CompilerParams(vmem_limit_bytes=32 * 1024 * 1024),
        cost_estimate=LIGHT,
        name="attend" + str(len(names)),
    )(band, q, *arrays, *(() if first else state))


def shards(queries, keys, values, band):
    barrier = lax.optimization_barrier
    *pieces, raw = pack(keys, values, queries)
    z4_raw = move(raw, from_z(4))
    own, q = join(over_heads(pieces))

    xnext, xprev = move(own, from_x(1)), move(own, from_x(-1))
    next1, prev1 = move(own, from_chip(1)), move(own, from_chip(-1))
    sent, z4_raw = barrier((own, z4_raw))
    partner = move(sent, FROM_PARTNER)
    z4_packed = unpack(z4_raw)
    z4 = lax.all_to_all(z4_packed, "head", split_axis=0, concat_axis=0, tiled=True)

    def step(state, last=False, **blocks):
        blocks = {k: b if isinstance(b, tuple) else ("joint", b) for k, b in blocks.items()}
        return attend(band, q, blocks, state, last)

    z = (lax.axis_index("frame") // CS) % ZS
    next2 = move(jnp.where(z < 2, xnext, own), from_z(2))
    prev2 = move(jnp.where(z >= ZS - 2, xprev, own), from_z(-2))
    z4x = move(z4, FROM_X_FOR_8)
    sent, sent1, sent2, *_ = barrier((own, next1, prev1, z4))
    x2 = move(sent, from_x(2))
    next1p, prev1p = move(sent1, FROM_PARTNER), move(sent2, FROM_PARTNER)
    state = step(None, own=own, xnext=xnext, xprev=xprev, z4=z4)
    next2, prev2, z4x, x2, state = barrier((next2, prev2, z4x, x2, state))
    next2p = move(next2, FROM_PARTNER)
    sent, _ = barrier((prev2, next2p))
    prev2p = move(sent, FROM_PARTNER)
    state = step(
        state, partner=partner, next1=next1, prev1=prev1, next1p=next1p, prev1p=prev1p
    )
    outs = step(
        state, True, x2=x2, z4x=z4x, next2=next2, prev2=prev2, far2p=("choice", prev2p, next2p)
    )
    return place(over_heads(outs))


def solution(mesh):
    placed = (
        P(("frame", "head"), None),
        P(("frame", "head"), None),
        P(("frame", "head"), None),
        P("frame", None),
    )
    return jax.shard_map(
        shards, mesh=mesh, in_specs=placed, out_specs=P(("frame", "head"), None), check_vma=False
    )
```

```python
import functools
import math

import jax
import jax.numpy as jnp
from jax import lax
from jax.experimental import pallas as pl
from jax.experimental.pallas import tpu as pltpu
from jax.sharding import PartitionSpec as P

HEAD_DIM = 128
TOK = 256
QUARTER = 64
HEADS_HERE = 3
W = HEADS_HERE * HEAD_DIM
XS, ZS, CS, YS = 4, 8, 2, 4
FRAMES = XS * ZS * CS
SCALE = HEAD_DIM**-0.5 * math.log2(math.e)
VMEM = pl.BlockSpec(memory_space=pltpu.VMEM)
LIGHT = pl.CostEstimate(flops=1, bytes_accessed=1, transcendentals=0)
SMEM = pl.BlockSpec(memory_space=pltpu.SMEM)


def frame_of(x, z, core):
    return ((x % XS) * ZS + z % ZS) * CS + core


def route(source):
    return [
        (frame_of(*source(x, z, c)), frame_of(x, z, c))
        for x in range(XS)
        for z in range(ZS)
        for c in range(CS)
    ]


def from_z(step):
    return route(lambda x, z, c: (x, z + step, c))


def from_x(step):
    return route(lambda x, z, c: (x + step, z, c))


def from_chip(step):
    return [((f + step * CS) % FRAMES, f) for f in range(FRAMES)]


FROM_PARTNER = route(lambda x, z, c: (x, z, 1 - c))
FROM_X_FOR_8 = route(lambda x, z, c: (x - 1 if z < ZS // 2 else x + 1, z, c))


def move(block, pairs):
    return lax.ppermute(block, "frame", pairs)


def copy_all(pairs):
    for source, out in pairs:
        out[...] = source[...]


def copier(kernel, out_shape, name):
    return lambda *arrays: pl.pallas_call(
        kernel,
        out_shape=out_shape,
        in_specs=[VMEM] * len(arrays),
        out_specs=[VMEM] * len(out_shape),
        cost_estimate=LIGHT,
        name=name,
    )(*arrays)


def bf16(rows, columns):
    return jax.ShapeDtypeStruct((rows, columns), jnp.bfloat16)


def group_at(group):
    return pl.ds(pl.multiple_of(group * W, W), W)


def quarter_at(quarter):
    return pl.ds(pl.multiple_of(quarter * QUARTER, QUARTER), QUARTER)


def pack_kernel(k_ref, v_ref, q_ref, p0, p1, p2, p3, raw_ref):
    y = lax.axis_index("head")
    pairs = []
    for step, out in enumerate((p0, p1, p2, p3)):
        for i, ref in enumerate((k_ref, v_ref, q_ref)):
            pairs.append((ref.at[:, group_at((y + step) % YS)], out.at[:, i * W : (i + 1) * W]))
    for i, ref in enumerate((k_ref, v_ref)):
        pairs.append((ref, raw_ref.at[:, i * YS * W : (i + 1) * YS * W]))
    copy_all(pairs)


def pack(keys, values, queries):
    out_shape = [bf16(QUARTER, 3 * W)] * YS + [bf16(QUARTER, 2 * YS * W)]
    return copier(pack_kernel, out_shape, "pack")(keys, values, queries)


def unpack_kernel(raw_ref, out_ref):
    pairs = []
    for g in range(YS):
        for i in range(2):
            at = (i * YS + g) * W
            out = out_ref.at[g * QUARTER : (g + 1) * QUARTER, i * W : (i + 1) * W]
            pairs.append((raw_ref.at[:, at : at + W], out))
    copy_all(pairs)


def unpack(raw):
    return copier(unpack_kernel, [bf16(TOK, 2 * W)], "unpack")(raw)[0]


def join_kernel(p0, p1, p2, p3, kv_ref, q_ref):
    y = lax.axis_index("head")
    pairs = []
    for step, piece in enumerate((p0, p1, p2, p3)):
        rows = quarter_at((y + YS - step) % YS)
        pairs.append((piece.at[:, : 2 * W], kv_ref.at[rows, :]))
        pairs.append((piece.at[:, 2 * W :], q_ref.at[rows, :]))
    copy_all(pairs)


def join(pieces):
    return copier(join_kernel, [bf16(TOK, 2 * W), bf16(TOK, W)], "join")(*pieces)


def place_kernel(p0, p1, p2, p3, out_ref):
    y = lax.axis_index("head")
    pairs = [
        (piece, out_ref.at[:, group_at((y + YS - step) % YS)])
        for step, piece in enumerate((p0, p1, p2, p3))
    ]
    copy_all(pairs)


def place(pieces):
    return copier(place_kernel, [bf16(QUARTER, YS * W)], "place")(*pieces)[0]


def y_from(step):
    return [((y - step) % YS, y) for y in range(YS)]


def over_heads(pieces):
    return [pieces[0]] + [lax.ppermute(pieces[s], "head", y_from(s)) for s in range(1, YS)]


BLOCKS = {
    "own": (lambda f, x, z, c: f, None),
    "partner": (lambda f, x, z, c: f + 1 - 2 * c, 128),
    "next1": (lambda f, x, z, c: f + 2, 64),
    "prev1": (lambda f, x, z, c: f - 2, 64),
    "next1p": (lambda f, x, z, c: f + 3 - 2 * c, 128),
    "prev1p": (lambda f, x, z, c: f - 1 - 2 * c, 128),
    "next2": (lambda f, x, z, c: f + 4, 32),
    "prev2": (lambda f, x, z, c: f - 4, 32),
    "far2p": (lambda f, x, z, c: f - 3 + 6 * c, 64),
    "z4": (lambda f, x, z, c: jnp.where(z < 4, f + 8, f - 8), 32),
    "z4x": (lambda f, x, z, c: jnp.where(z < 4, f - 8, f + 8), 32),
    "xnext": (lambda f, x, z, c: f + 16, 32),
    "xprev": (lambda f, x, z, c: f - 16, 32),
    "x2": (lambda f, x, z, c: jnp.where(x < 2, f + 32, f - 32), 32),
}
ROWS = 128
HALF = 64
FAR_STARTS = (0, 32, 96, 128)


def dot_t(a, b):
    return lax.dot_general(a, b, (((1,), (1,)), ((), ())), preferred_element_type=jnp.float32)


def attend_kernel(names, kinds, first, last, band_ref, q_ref, *refs):
    core = lax.axis_index("frame") % CS
    blocks, at = [], 0
    for kind in kinds:
        blocks.append(refs[at : at + (1 if kind == "joint" else 2)])
        at += len(blocks[-1])
    refs = refs[at:]

    def block(i, rows, columns, value):
        kind, parts = kinds[i], blocks[i]
        if kind == "split":
            return parts[value][rows, columns]
        columns = slice(columns.start + value * W, columns.stop + value * W)
        here = parts[0][rows, columns]
        if kind == "choice":
            here = jnp.where(core == 0, here, parts[1][rows, columns])
        return here

    whole = slice(0, TOK)
    if not first:
        stats_in, acc_in = refs[:2]
        refs = refs[2:]
    f = lax.axis_index("frame")
    x, z = f // (ZS * CS), (f // CS) % ZS
    bands = []
    for name in names:
        frame_at, reach = BLOCKS[name]
        if reach is None:
            bands.append(None)
            continue
        g = frame_at(f, x, z, core)
        inside = (g >= 0) & (g < FRAMES)
        bands.append(jnp.where(inside, band_ref[0, jnp.clip(g, 0, FRAMES - 1)], -1))
    far = [i for i, n in enumerate(names) if BLOCKS[n][1] == 32]
    near = [i for i in range(len(names)) if i not in far]
    gaps = {}
    for part in range(TOK // ROWS):
        row0 = part * ROWS
        gap = lax.broadcasted_iota(jnp.int32, (ROWS, TOK), 0) - lax.broadcasted_iota(
            jnp.int32, (ROWS, TOK), 1
        )
        starts = FAR_STARTS[part * 2 : part * 2 + 2]
        far_gap = lax.broadcasted_iota(jnp.int32, (HALF, ROWS), 0) - lax.broadcasted_iota(
            jnp.int32, (HALF, ROWS), 1
        )
        gaps[part] = (
            jnp.abs(gap + row0),
            jnp.abs(
                jnp.concatenate([far_gap + (row0 + j * HALF - starts[j]) for j in range(2)], axis=0)
            ),
            starts,
        )

    units = [(part, h) for part in range(TOK // ROWS) for h in range(HEADS_HERE)]
    size = len(units) if len(names) <= 2 else HEADS_HERE
    for u0 in range(0, len(units), size):
        group = units[u0 : u0 + size]
        tiles, tops, fades, ps, totals, outs = {}, {}, {}, {}, {}, {}
        for u in group:
            part, h = u
            near_gap, far_gap, starts = gaps[part]
            rows = slice(part * ROWS, (part + 1) * ROWS)
            kc = slice(h * HEAD_DIM, (h + 1) * HEAD_DIM)
            q = q_ref[rows, kc]
            for i in near:
                s = dot_t(q, block(i, whole, kc, 0)) * SCALE
                if bands[i] is not None:
                    s = jnp.where(near_gap <= bands[i], s, -jnp.inf)
                tiles[u, i] = s
            for i in far:
                s = [
                    dot_t(
                        q[j * HALF : (j + 1) * HALF],
                        block(i, slice(starts[j], starts[j] + ROWS), kc, 0),
                    )
                    for j in range(2)
                ]
                s = jnp.concatenate(s, axis=0) * SCALE
                tiles[u, i] = jnp.where(far_gap <= bands[i], s, -jnp.inf)
        for u in group:
            parts = [
                tiles[u, i][:, c0 : c0 + 128]
                for i in range(len(names))
                for c0 in range(0, tiles[u, i].shape[1], 128)
            ]
            tops[u] = jnp.max(functools.reduce(jnp.maximum, parts), axis=1, keepdims=True)
        if not first:
            for u in group:
                part, h = u
                rows = slice(part * ROWS, (part + 1) * ROWS)
                top_in = stats_in[rows, h : h + 1]
                tops[u] = jnp.maximum(tops[u], top_in)
                fades[u] = jnp.exp2(top_in - tops[u])
        for u in group:
            parts = []
            for i in range(len(names)):
                p = jnp.exp2(tiles[u, i] - tops[u])
                parts += [p[:, c0 : c0 + 128] for c0 in range(0, p.shape[1], 128)]
                ps[u, i] = p.astype(jnp.bfloat16)
            totals[u] = jnp.sum(functools.reduce(jnp.add, parts), axis=1, keepdims=True)
        for u in group:
            part, h = u
            starts = gaps[part][2]
            kc = slice(h * HEAD_DIM, (h + 1) * HEAD_DIM)
            parts = []
            for i in range(len(names)):
                p = ps[u, i]
                if i in near:
                    o = jnp.dot(p, block(i, whole, kc, 1), preferred_element_type=jnp.float32)
                else:
                    o = [
                        jnp.dot(
                            p[j * HALF : (j + 1) * HALF],
                            block(i, slice(starts[j], starts[j] + ROWS), kc, 1),
                            preferred_element_type=jnp.float32,
                        )
                        for j in range(2)
                    ]
                    o = jnp.concatenate(o, axis=0)
                parts.append(o)
            outs[u] = functools.reduce(jnp.add, parts)
        for u in group:
            part, h = u
            rows = slice(part * ROWS, (part + 1) * ROWS)
            kc = slice(h * HEAD_DIM, (h + 1) * HEAD_DIM)
            total, out = totals[u], outs[u]
            if not first:
                total = total + stats_in[rows, 4 + h : 5 + h] * fades[u]
                out = out + acc_in[rows, kc] * fades[u]
            if last:
                refs[YS][rows, kc] = (out * (1.0 / total)).astype(jnp.bfloat16)
            else:
                refs[0][rows, h : h + 1] = tops[u]
                refs[0][rows, 4 + h : 5 + h] = total
                refs[1][rows, kc] = out
    if last:
        y = lax.axis_index("head")
        for step in range(YS):
            rows = pl.ds(pl.multiple_of(((y + step) % YS) * QUARTER, QUARTER), QUARTER)
            refs[step][...] = refs[YS][rows, :]


def attend(band, q, blocks, state, last):
    names = list(blocks)
    first = state is None
    kinds, arrays = [], []
    for block in blocks.values():
        kinds.append(block[0])
        arrays += block[1:]
    if last:
        out_shape = [jax.ShapeDtypeStruct((QUARTER, W), jnp.bfloat16)] * YS
    else:
        out_shape = [
            jax.ShapeDtypeStruct((TOK, 128), jnp.float32),
            jax.ShapeDtypeStruct((TOK, W), jnp.float32),
        ]
    return pl.pallas_call(
        functools.partial(attend_kernel, names, kinds, first, last),
        out_shape=out_shape,
        in_specs=[SMEM] + [VMEM] * (1 + len(arrays) + (0 if first else 2)),
        out_specs=[VMEM] * len(out_shape),
        scratch_shapes=[pltpu.VMEM((TOK, W), jnp.bfloat16)] if last else [],
        compiler_params=pltpu.CompilerParams(vmem_limit_bytes=32 * 1024 * 1024),
        cost_estimate=LIGHT,
        name="attend" + str(len(names)),
    )(band, q, *arrays, *(() if first else state))


def shards(queries, keys, values, band):
    barrier = lax.optimization_barrier
    *pieces, raw = pack(keys, values, queries)
    z4_raw = move(raw, from_z(4))
    own, q = join(over_heads(pieces))

    xnext, xprev = move(own, from_x(1)), move(own, from_x(-1))
    next1, prev1 = move(own, from_chip(1)), move(own, from_chip(-1))
    sent, z4_raw = barrier((own, z4_raw))
    partner = move(sent, FROM_PARTNER)
    z4_packed = unpack(z4_raw)
    z4 = lax.all_to_all(z4_packed, "head", split_axis=0, concat_axis=0, tiled=True)

    def step(state, last=False, **blocks):
        blocks = {k: b if isinstance(b, tuple) else ("joint", b) for k, b in blocks.items()}
        return attend(band, q, blocks, state, last)

    z = (lax.axis_index("frame") // CS) % ZS
    next2 = move(jnp.where(z < 2, xnext, own), from_z(2))
    prev2 = move(jnp.where(z >= ZS - 2, xprev, own), from_z(-2))
    z4x = move(z4, FROM_X_FOR_8)
    sent, sent1, sent2, *_ = barrier((own, next1, prev1, z4))
    x2 = move(sent, from_x(2))
    next1p, prev1p = move(sent1, FROM_PARTNER), move(sent2, FROM_PARTNER)
    state = step(None, own=own, xnext=xnext, xprev=xprev, z4=z4, next1=next1, prev1=prev1)
    next2, prev2, z4x, x2, state = barrier((next2, prev2, z4x, x2, state))
    next2p = move(next2, FROM_PARTNER)
    sent, _ = barrier((prev2, next2p))
    prev2p = move(sent, FROM_PARTNER)
    outs = step(
        state,
        True,
        partner=partner,
        next1p=next1p,
        prev1p=prev1p,
        x2=x2,
        z4x=z4x,
        next2=next2,
        prev2=prev2,
        far2p=("choice", prev2p, next2p),
    )
    return place(over_heads(outs))


def solution(mesh):
    placed = (
        P(("frame", "head"), None),
        P(("frame", "head"), None),
        P(("frame", "head"), None),
        P("frame", None),
    )
    return jax.shard_map(
        shards, mesh=mesh, in_specs=placed, out_specs=P(("frame", "head"), None), check_vma=False
    )
```

```python
import functools
import math

import jax
import jax.numpy as jnp
from jax import lax
from jax.experimental import pallas as pl
from jax.experimental.pallas import tpu as pltpu
from jax.sharding import PartitionSpec as P

HEAD_DIM = 128
TOK = 256
QUARTER = 64
HEADS_HERE = 3
W = HEADS_HERE * HEAD_DIM
XS, ZS, CS, YS = 4, 8, 2, 4
FRAMES = XS * ZS * CS
SCALE = HEAD_DIM**-0.5 * math.log2(math.e)
VMEM = pl.BlockSpec(memory_space=pltpu.VMEM)
LIGHT = pl.CostEstimate(flops=1, bytes_accessed=1, transcendentals=0)
SMEM = pl.BlockSpec(memory_space=pltpu.SMEM)


def frame_of(x, z, core):
    return ((x % XS) * ZS + z % ZS) * CS + core


def route(source):
    return [
        (frame_of(*source(x, z, c)), frame_of(x, z, c))
        for x in range(XS)
        for z in range(ZS)
        for c in range(CS)
    ]


def from_z(step):
    return route(lambda x, z, c: (x, z + step, c))


def from_x(step):
    return route(lambda x, z, c: (x + step, z, c))


def from_chip(step):
    return [((f + step * CS) % FRAMES, f) for f in range(FRAMES)]


FROM_PARTNER = route(lambda x, z, c: (x, z, 1 - c))
FROM_X_FOR_8 = route(lambda x, z, c: (x - 1 if z < ZS // 2 else x + 1, z, c))


def move(block, pairs):
    return lax.ppermute(block, "frame", pairs)


def copy_all(pairs):
    for source, out in pairs:
        out[...] = source[...]


def copier(kernel, out_shape, name):
    return lambda *arrays: pl.pallas_call(
        kernel,
        out_shape=out_shape,
        in_specs=[VMEM] * len(arrays),
        out_specs=[VMEM] * len(out_shape),
        cost_estimate=LIGHT,
        name=name,
    )(*arrays)


def bf16(rows, columns):
    return jax.ShapeDtypeStruct((rows, columns), jnp.bfloat16)


def group_at(group):
    return pl.ds(pl.multiple_of(group * W, W), W)


def quarter_at(quarter):
    return pl.ds(pl.multiple_of(quarter * QUARTER, QUARTER), QUARTER)


def pack_kernel(k_ref, v_ref, q_ref, p0, p1, p2, p3, raw_ref):
    y = lax.axis_index("head")
    pairs = []
    for step, out in enumerate((p0, p1, p2, p3)):
        for i, ref in enumerate((k_ref, v_ref, q_ref)):
            pairs.append((ref.at[:, group_at((y + step) % YS)], out.at[:, i * W : (i + 1) * W]))
    for i, ref in enumerate((k_ref, v_ref)):
        pairs.append((ref, raw_ref.at[:, i * YS * W : (i + 1) * YS * W]))
    copy_all(pairs)


def pack(keys, values, queries):
    out_shape = [bf16(QUARTER, 3 * W)] * YS + [bf16(QUARTER, 2 * YS * W)]
    return copier(pack_kernel, out_shape, "pack")(keys, values, queries)


def unpack_kernel(raw_ref, out_ref):
    pairs = []
    for g in range(YS):
        for i in range(2):
            at = (i * YS + g) * W
            out = out_ref.at[g * QUARTER : (g + 1) * QUARTER, i * W : (i + 1) * W]
            pairs.append((raw_ref.at[:, at : at + W], out))
    copy_all(pairs)


def unpack(raw):
    return copier(unpack_kernel, [bf16(TOK, 2 * W)], "unpack")(raw)[0]


def join_kernel(p0, p1, p2, p3, kv_ref, q_ref):
    y = lax.axis_index("head")
    pairs = []
    for step, piece in enumerate((p0, p1, p2, p3)):
        rows = quarter_at((y + YS - step) % YS)
        pairs.append((piece.at[:, : 2 * W], kv_ref.at[rows, :]))
        pairs.append((piece.at[:, 2 * W :], q_ref.at[rows, :]))
    copy_all(pairs)


def join(pieces):
    return copier(join_kernel, [bf16(TOK, 2 * W), bf16(TOK, W)], "join")(*pieces)


def place_kernel(p0, p1, p2, p3, out_ref):
    y = lax.axis_index("head")
    pairs = [
        (piece, out_ref.at[:, group_at((y + YS - step) % YS)])
        for step, piece in enumerate((p0, p1, p2, p3))
    ]
    copy_all(pairs)


def place(pieces):
    return copier(place_kernel, [bf16(QUARTER, YS * W)], "place")(*pieces)[0]


def y_from(step):
    return [((y - step) % YS, y) for y in range(YS)]


def over_heads(pieces):
    return [pieces[0]] + [lax.ppermute(pieces[s], "head", y_from(s)) for s in range(1, YS)]


BLOCKS = {
    "own": (lambda f, x, z, c: f, None),
    "partner": (lambda f, x, z, c: f + 1 - 2 * c, 128),
    "next1": (lambda f, x, z, c: f + 2, 64),
    "prev1": (lambda f, x, z, c: f - 2, 64),
    "next1p": (lambda f, x, z, c: f + 3 - 2 * c, 128),
    "prev1p": (lambda f, x, z, c: f - 1 - 2 * c, 128),
    "next2": (lambda f, x, z, c: f + 4, 32),
    "prev2": (lambda f, x, z, c: f - 4, 32),
    "far2p": (lambda f, x, z, c: f - 3 + 6 * c, 64),
    "z4": (lambda f, x, z, c: jnp.where(z < 4, f + 8, f - 8), 32),
    "z4x": (lambda f, x, z, c: jnp.where(z < 4, f - 8, f + 8), 32),
    "xnext": (lambda f, x, z, c: f + 16, 32),
    "xprev": (lambda f, x, z, c: f - 16, 32),
    "x2": (lambda f, x, z, c: jnp.where(x < 2, f + 32, f - 32), 32),
}
ROWS = 128
HALF = 64
FAR_STARTS = (0, 32, 96, 128)


def dot_t(a, b):
    return lax.dot_general(a, b, (((1,), (1,)), ((), ())), preferred_element_type=jnp.float32)


def attend_kernel(names, kinds, first, last, band_ref, q_ref, *refs):
    core = lax.axis_index("frame") % CS
    blocks, at = [], 0
    for kind in kinds:
        blocks.append(refs[at : at + (1 if kind == "joint" else 2)])
        at += len(blocks[-1])
    refs = refs[at:]

    def block(i, rows, columns, value):
        kind, parts = kinds[i], blocks[i]
        if kind == "split":
            return parts[value][rows, columns]
        columns = slice(columns.start + value * W, columns.stop + value * W)
        here = parts[0][rows, columns]
        if kind == "choice":
            here = jnp.where(core == 0, here, parts[1][rows, columns])
        return here

    whole = slice(0, TOK)
    if not first:
        stats_in, acc_in = refs[:2]
        refs = refs[2:]
    f = lax.axis_index("frame")
    x, z = f // (ZS * CS), (f // CS) % ZS
    bands = []
    for name in names:
        frame_at, reach = BLOCKS[name]
        if reach is None:
            bands.append(None)
            continue
        g = frame_at(f, x, z, core)
        inside = (g >= 0) & (g < FRAMES)
        bands.append(jnp.where(inside, band_ref[0, jnp.clip(g, 0, FRAMES - 1)], -1))
    far = [i for i, n in enumerate(names) if BLOCKS[n][1] == 32]
    near = [i for i in range(len(names)) if i not in far]
    gaps = {}
    for part in range(TOK // ROWS):
        row0 = part * ROWS
        gap = lax.broadcasted_iota(jnp.int32, (ROWS, TOK), 0) - lax.broadcasted_iota(
            jnp.int32, (ROWS, TOK), 1
        )
        starts = FAR_STARTS[part * 2 : part * 2 + 2]
        far_gap = lax.broadcasted_iota(jnp.int32, (HALF, ROWS), 0) - lax.broadcasted_iota(
            jnp.int32, (HALF, ROWS), 1
        )
        gaps[part] = (
            jnp.abs(gap + row0),
            jnp.abs(
                jnp.concatenate([far_gap + (row0 + j * HALF - starts[j]) for j in range(2)], axis=0)
            ),
            starts,
        )

    units = [(part, h) for part in range(TOK // ROWS) for h in range(HEADS_HERE)]
    size = len(units) if len(names) <= 2 else HEADS_HERE
    for u0 in range(0, len(units), size):
        group = units[u0 : u0 + size]
        tiles, tops, fades, ps, totals, outs = {}, {}, {}, {}, {}, {}
        for u in group:
            part, h = u
            near_gap, far_gap, starts = gaps[part]
            rows = slice(part * ROWS, (part + 1) * ROWS)
            kc = slice(h * HEAD_DIM, (h + 1) * HEAD_DIM)
            q = q_ref[rows, kc]
            for i in near:
                s = dot_t(q, block(i, whole, kc, 0)) * SCALE
                if bands[i] is not None:
                    s = jnp.where(near_gap <= bands[i], s, -jnp.inf)
                tiles[u, i] = s
            for i in far:
                s = [
                    dot_t(
                        q[j * HALF : (j + 1) * HALF],
                        block(i, slice(starts[j], starts[j] + ROWS), kc, 0),
                    )
                    for j in range(2)
                ]
                s = jnp.concatenate(s, axis=0) * SCALE
                tiles[u, i] = jnp.where(far_gap <= bands[i], s, -jnp.inf)
        for u in group:
            parts = [
                tiles[u, i][:, c0 : c0 + 128]
                for i in range(len(names))
                for c0 in range(0, tiles[u, i].shape[1], 128)
            ]
            tops[u] = jnp.max(functools.reduce(jnp.maximum, parts), axis=1, keepdims=True)
        if not first:
            for u in group:
                part, h = u
                rows = slice(part * ROWS, (part + 1) * ROWS)
                top_in = stats_in[rows, h : h + 1]
                tops[u] = jnp.maximum(tops[u], top_in)
                fades[u] = jnp.exp2(top_in - tops[u])
        for u in group:
            parts = []
            for i in range(len(names)):
                p = jnp.exp2(tiles[u, i] - tops[u])
                parts += [p[:, c0 : c0 + 128] for c0 in range(0, p.shape[1], 128)]
                ps[u, i] = p.astype(jnp.bfloat16)
            totals[u] = jnp.sum(functools.reduce(jnp.add, parts), axis=1, keepdims=True)
        for u in group:
            part, h = u
            starts = gaps[part][2]
            kc = slice(h * HEAD_DIM, (h + 1) * HEAD_DIM)
            parts = []
            for i in range(len(names)):
                p = ps[u, i]
                if i in near:
                    o = jnp.dot(p, block(i, whole, kc, 1), preferred_element_type=jnp.float32)
                else:
                    o = [
                        jnp.dot(
                            p[j * HALF : (j + 1) * HALF],
                            block(i, slice(starts[j], starts[j] + ROWS), kc, 1),
                            preferred_element_type=jnp.float32,
                        )
                        for j in range(2)
                    ]
                    o = jnp.concatenate(o, axis=0)
                parts.append(o)
            outs[u] = functools.reduce(jnp.add, parts)
        for u in group:
            part, h = u
            rows = slice(part * ROWS, (part + 1) * ROWS)
            kc = slice(h * HEAD_DIM, (h + 1) * HEAD_DIM)
            total, out = totals[u], outs[u]
            if not first:
                total = total + stats_in[rows, 4 + h : 5 + h] * fades[u]
                out = out + acc_in[rows, kc] * fades[u]
            if last:
                refs[YS][rows, kc] = (out * (1.0 / total)).astype(jnp.bfloat16)
            else:
                refs[0][rows, h : h + 1] = tops[u]
                refs[0][rows, 4 + h : 5 + h] = total
                refs[1][rows, kc] = out
    if last:
        y = lax.axis_index("head")
        for step in range(YS):
            rows = pl.ds(pl.multiple_of(((y + step) % YS) * QUARTER, QUARTER), QUARTER)
            refs[step][...] = refs[YS][rows, :]


def attend(band, q, blocks, state, last):
    names = list(blocks)
    first = state is None
    kinds, arrays = [], []
    for block in blocks.values():
        kinds.append(block[0])
        arrays += block[1:]
    if last:
        out_shape = [jax.ShapeDtypeStruct((QUARTER, W), jnp.bfloat16)] * YS
    else:
        out_shape = [
            jax.ShapeDtypeStruct((TOK, 128), jnp.float32),
            jax.ShapeDtypeStruct((TOK, W), jnp.float32),
        ]
    return pl.pallas_call(
        functools.partial(attend_kernel, names, kinds, first, last),
        out_shape=out_shape,
        in_specs=[SMEM] + [VMEM] * (1 + len(arrays) + (0 if first else 2)),
        out_specs=[VMEM] * len(out_shape),
        scratch_shapes=[pltpu.VMEM((TOK, W), jnp.bfloat16)] if last else [],
        compiler_params=pltpu.CompilerParams(vmem_limit_bytes=32 * 1024 * 1024),
        cost_estimate=LIGHT,
        name="attend" + str(len(names)),
    )(band, q, *arrays, *(() if first else state))


def shards(queries, keys, values, band):
    barrier = lax.optimization_barrier
    *pieces, raw = pack(keys, values, queries)
    z4_raw = move(raw, from_z(4))
    own, q = join(over_heads(pieces))

    xnext, xprev = move(own, from_x(1)), move(own, from_x(-1))
    next1, prev1 = move(own, from_chip(1)), move(own, from_chip(-1))
    sent, z4_raw = barrier((own, z4_raw))
    partner = move(sent, FROM_PARTNER)
    z4_packed = unpack(z4_raw)
    z4 = lax.all_to_all(z4_packed, "head", split_axis=0, concat_axis=0, tiled=True)

    def step(state, last=False, **blocks):
        blocks = {k: b if isinstance(b, tuple) else ("joint", b) for k, b in blocks.items()}
        return attend(band, q, blocks, state, last)

    z = (lax.axis_index("frame") // CS) % ZS
    next2 = move(jnp.where(z < 2, xnext, own), from_z(2))
    prev2 = move(jnp.where(z >= ZS - 2, xprev, own), from_z(-2))
    z4x = move(z4, FROM_X_FOR_8)
    sent, sent1, sent2, *_ = barrier((own, next1, prev1, z4))
    x2 = move(sent, from_x(2))
    next1p, prev1p = move(sent1, FROM_PARTNER), move(sent2, FROM_PARTNER)
    state = step(
        None, own=own, partner=partner, xnext=xnext, xprev=xprev, z4=z4, next1=next1, prev1=prev1
    )
    next2, prev2, z4x, x2, state = barrier((next2, prev2, z4x, x2, state))
    next2p = move(next2, FROM_PARTNER)
    sent, _ = barrier((prev2, next2p))
    prev2p = move(sent, FROM_PARTNER)
    outs = step(
        state,
        True,
        next1p=next1p,
        prev1p=prev1p,
        x2=x2,
        z4x=z4x,
        next2=next2,
        prev2=prev2,
        far2p=("choice", prev2p, next2p),
    )
    return place(over_heads(outs))


def solution(mesh):
    placed = (
        P(("frame", "head"), None),
        P(("frame", "head"), None),
        P(("frame", "head"), None),
        P("frame", None),
    )
    return jax.shard_map(
        shards, mesh=mesh, in_specs=placed, out_specs=P(("frame", "head"), None), check_vma=False
    )
```

```python
import functools
import math

import jax
import jax.numpy as jnp
from jax import lax
from jax.experimental import pallas as pl
from jax.experimental.pallas import tpu as pltpu
from jax.sharding import PartitionSpec as P

HEAD_DIM = 128
TOK = 256
QUARTER = 64
HEADS_HERE = 3
W = HEADS_HERE * HEAD_DIM
XS, ZS, CS, YS = 4, 8, 2, 4
FRAMES = XS * ZS * CS
SCALE = HEAD_DIM**-0.5 * math.log2(math.e)
VMEM = pl.BlockSpec(memory_space=pltpu.VMEM)
LIGHT = pl.CostEstimate(flops=1, bytes_accessed=1, transcendentals=0)
SMEM = pl.BlockSpec(memory_space=pltpu.SMEM)


def frame_of(x, z, core):
    return ((x % XS) * ZS + z % ZS) * CS + core


def route(source):
    return [
        (frame_of(*source(x, z, c)), frame_of(x, z, c))
        for x in range(XS)
        for z in range(ZS)
        for c in range(CS)
    ]


def from_z(step):
    return route(lambda x, z, c: (x, z + step, c))


def from_x(step):
    return route(lambda x, z, c: (x + step, z, c))


def from_chip(step):
    return [((f + step * CS) % FRAMES, f) for f in range(FRAMES)]


FROM_PARTNER = route(lambda x, z, c: (x, z, 1 - c))
FROM_X_FOR_8 = route(lambda x, z, c: (x - 1 if z < ZS // 2 else x + 1, z, c))


def move(block, pairs):
    return lax.ppermute(block, "frame", pairs)


def copy_all(pairs):
    for source, out in pairs:
        out[...] = source[...]


def copier(kernel, out_shape, name):
    return lambda *arrays: pl.pallas_call(
        kernel,
        out_shape=out_shape,
        in_specs=[VMEM] * len(arrays),
        out_specs=[VMEM] * len(out_shape),
        cost_estimate=LIGHT,
        name=name,
    )(*arrays)


def bf16(rows, columns):
    return jax.ShapeDtypeStruct((rows, columns), jnp.bfloat16)


def group_at(group):
    return pl.ds(pl.multiple_of(group * W, W), W)


def quarter_at(quarter):
    return pl.ds(pl.multiple_of(quarter * QUARTER, QUARTER), QUARTER)


def pack_kernel(k_ref, v_ref, q_ref, p0, p1, p2, p3, raw_ref):
    y = lax.axis_index("head")
    pairs = []
    for step, out in enumerate((p0, p1, p2, p3)):
        for i, ref in enumerate((k_ref, v_ref, q_ref)):
            pairs.append((ref.at[:, group_at((y + step) % YS)], out.at[:, i * W : (i + 1) * W]))
    for i, ref in enumerate((k_ref, v_ref)):
        pairs.append((ref, raw_ref.at[:, i * YS * W : (i + 1) * YS * W]))
    copy_all(pairs)


def pack(keys, values, queries):
    out_shape = [bf16(QUARTER, 3 * W)] * YS + [bf16(QUARTER, 2 * YS * W)]
    return copier(pack_kernel, out_shape, "pack")(keys, values, queries)


def unpack_kernel(raw_ref, out_ref):
    pairs = []
    for g in range(YS):
        for i in range(2):
            at = (i * YS + g) * W
            out = out_ref.at[g * QUARTER : (g + 1) * QUARTER, i * W : (i + 1) * W]
            pairs.append((raw_ref.at[:, at : at + W], out))
    copy_all(pairs)


def unpack(raw):
    return copier(unpack_kernel, [bf16(TOK, 2 * W)], "unpack")(raw)[0]


def join_kernel(p0, p1, p2, p3, kv_ref, q_ref):
    y = lax.axis_index("head")
    pairs = []
    for step, piece in enumerate((p0, p1, p2, p3)):
        rows = quarter_at((y + YS - step) % YS)
        pairs.append((piece.at[:, : 2 * W], kv_ref.at[rows, :]))
        pairs.append((piece.at[:, 2 * W :], q_ref.at[rows, :]))
    copy_all(pairs)


def join(pieces):
    return copier(join_kernel, [bf16(TOK, 2 * W), bf16(TOK, W)], "join")(*pieces)


def place_kernel(p0, p1, p2, p3, out_ref):
    y = lax.axis_index("head")
    pairs = [
        (piece, out_ref.at[:, group_at((y + YS - step) % YS)])
        for step, piece in enumerate((p0, p1, p2, p3))
    ]
    copy_all(pairs)


def place(pieces):
    return copier(place_kernel, [bf16(QUARTER, YS * W)], "place")(*pieces)[0]


def y_from(step):
    return [((y - step) % YS, y) for y in range(YS)]


def over_heads(pieces):
    return [pieces[0]] + [lax.ppermute(pieces[s], "head", y_from(s)) for s in range(1, YS)]


BLOCKS = {
    "own": (lambda f, x, z, c: f, None),
    "partner": (lambda f, x, z, c: f + 1 - 2 * c, 128),
    "next1": (lambda f, x, z, c: f + 2, 64),
    "prev1": (lambda f, x, z, c: f - 2, 64),
    "next1p": (lambda f, x, z, c: f + 3 - 2 * c, 128),
    "prev1p": (lambda f, x, z, c: f - 1 - 2 * c, 128),
    "next2": (lambda f, x, z, c: f + 4, 32),
    "prev2": (lambda f, x, z, c: f - 4, 32),
    "far2p": (lambda f, x, z, c: f - 3 + 6 * c, 64),
    "z4": (lambda f, x, z, c: jnp.where(z < 4, f + 8, f - 8), 32),
    "z4x": (lambda f, x, z, c: jnp.where(z < 4, f - 8, f + 8), 32),
    "xnext": (lambda f, x, z, c: f + 16, 32),
    "xprev": (lambda f, x, z, c: f - 16, 32),
    "x2": (lambda f, x, z, c: jnp.where(x < 2, f + 32, f - 32), 32),
}
ROWS = 128
HALF = 64
FAR_STARTS = (0, 32, 96, 128)


def dot_t(a, b):
    return lax.dot_general(a, b, (((1,), (1,)), ((), ())), preferred_element_type=jnp.float32)


def attend_kernel(names, kinds, first, last, band_ref, q_ref, *refs):
    core = lax.axis_index("frame") % CS
    blocks, at = [], 0
    for kind in kinds:
        blocks.append(refs[at : at + (1 if kind == "joint" else 2)])
        at += len(blocks[-1])
    refs = refs[at:]

    def block(i, rows, columns, value):
        kind, parts = kinds[i], blocks[i]
        if kind == "split":
            return parts[value][rows, columns]
        columns = slice(columns.start + value * W, columns.stop + value * W)
        here = parts[0][rows, columns]
        if kind == "choice":
            here = jnp.where(core == 0, here, parts[1][rows, columns])
        return here

    whole = slice(0, TOK)
    if not first:
        stats_in, acc_in = refs[:2]
        refs = refs[2:]
    f = lax.axis_index("frame")
    x, z = f // (ZS * CS), (f // CS) % ZS
    bands = []
    for name in names:
        frame_at, reach = BLOCKS[name]
        if reach is None:
            bands.append(None)
            continue
        g = frame_at(f, x, z, core)
        inside = (g >= 0) & (g < FRAMES)
        bands.append(jnp.where(inside, band_ref[0, jnp.clip(g, 0, FRAMES - 1)], -1))
    far = [i for i, n in enumerate(names) if BLOCKS[n][1] == 32]
    near = [i for i in range(len(names)) if i not in far]
    gaps = {}
    for part in range(TOK // ROWS):
        row0 = part * ROWS
        gap = lax.broadcasted_iota(jnp.int32, (ROWS, TOK), 0) - lax.broadcasted_iota(
            jnp.int32, (ROWS, TOK), 1
        )
        starts = FAR_STARTS[part * 2 : part * 2 + 2]
        far_gap = lax.broadcasted_iota(jnp.int32, (HALF, ROWS), 0) - lax.broadcasted_iota(
            jnp.int32, (HALF, ROWS), 1
        )
        gaps[part] = (
            jnp.abs(gap + row0),
            jnp.abs(
                jnp.concatenate([far_gap + (row0 + j * HALF - starts[j]) for j in range(2)], axis=0)
            ),
            starts,
        )

    units = [(part, h) for part in range(TOK // ROWS) for h in range(HEADS_HERE)]
    size = len(units) if len(names) <= 2 else HEADS_HERE
    for u0 in range(0, len(units), size):
        group = units[u0 : u0 + size]
        tiles, tops, fades, ps, totals, outs = {}, {}, {}, {}, {}, {}
        for u in group:
            part, h = u
            near_gap, far_gap, starts = gaps[part]
            rows = slice(part * ROWS, (part + 1) * ROWS)
            kc = slice(h * HEAD_DIM, (h + 1) * HEAD_DIM)
            q = q_ref[rows, kc]
            for i in near:
                s = dot_t(q, block(i, whole, kc, 0)) * SCALE
                if bands[i] is not None:
                    s = jnp.where(near_gap <= bands[i], s, -jnp.inf)
                tiles[u, i] = s
            for i in far:
                s = [
                    dot_t(
                        q[j * HALF : (j + 1) * HALF],
                        block(i, slice(starts[j], starts[j] + ROWS), kc, 0),
                    )
                    for j in range(2)
                ]
                s = jnp.concatenate(s, axis=0) * SCALE
                tiles[u, i] = jnp.where(far_gap <= bands[i], s, -jnp.inf)
        for u in group:
            parts = [
                tiles[u, i][:, c0 : c0 + 128]
                for i in range(len(names))
                for c0 in range(0, tiles[u, i].shape[1], 128)
            ]
            tops[u] = jnp.max(functools.reduce(jnp.maximum, parts), axis=1, keepdims=True)
        if not first:
            for u in group:
                part, h = u
                rows = slice(part * ROWS, (part + 1) * ROWS)
                top_in = stats_in[rows, h : h + 1]
                tops[u] = jnp.maximum(tops[u], top_in)
                fades[u] = jnp.exp2(top_in - tops[u])
        for u in group:
            parts = []
            for i in range(len(names)):
                p = jnp.exp2(tiles[u, i] - tops[u])
                parts += [p[:, c0 : c0 + 128] for c0 in range(0, p.shape[1], 128)]
                ps[u, i] = p.astype(jnp.bfloat16)
            totals[u] = jnp.sum(functools.reduce(jnp.add, parts), axis=1, keepdims=True)
        for u in group:
            part, h = u
            starts = gaps[part][2]
            kc = slice(h * HEAD_DIM, (h + 1) * HEAD_DIM)
            parts = []
            for i in range(len(names)):
                p = ps[u, i]
                if i in near:
                    o = jnp.dot(p, block(i, whole, kc, 1), preferred_element_type=jnp.float32)
                else:
                    o = [
                        jnp.dot(
                            p[j * HALF : (j + 1) * HALF],
                            block(i, slice(starts[j], starts[j] + ROWS), kc, 1),
                            preferred_element_type=jnp.float32,
                        )
                        for j in range(2)
                    ]
                    o = jnp.concatenate(o, axis=0)
                parts.append(o)
            outs[u] = functools.reduce(jnp.add, parts)
        for u in group:
            part, h = u
            rows = slice(part * ROWS, (part + 1) * ROWS)
            kc = slice(h * HEAD_DIM, (h + 1) * HEAD_DIM)
            total, out = totals[u], outs[u]
            if not first:
                total = total + stats_in[rows, 4 + h : 5 + h] * fades[u]
                out = out + acc_in[rows, kc] * fades[u]
            if last:
                refs[YS][rows, kc] = (out * (1.0 / total)).astype(jnp.bfloat16)
            else:
                refs[0][rows, h : h + 1] = tops[u]
                refs[0][rows, 4 + h : 5 + h] = total
                refs[1][rows, kc] = out
    if last:
        y = lax.axis_index("head")
        for step in range(YS):
            rows = pl.ds(pl.multiple_of(((y + step) % YS) * QUARTER, QUARTER), QUARTER)
            refs[step][...] = refs[YS][rows, :]


def attend(band, q, blocks, state, last):
    names = list(blocks)
    first = state is None
    kinds, arrays = [], []
    for block in blocks.values():
        kinds.append(block[0])
        arrays += block[1:]
    if last:
        out_shape = [jax.ShapeDtypeStruct((QUARTER, W), jnp.bfloat16)] * YS
    else:
        out_shape = [
            jax.ShapeDtypeStruct((TOK, 128), jnp.float32),
            jax.ShapeDtypeStruct((TOK, W), jnp.float32),
        ]
    return pl.pallas_call(
        functools.partial(attend_kernel, names, kinds, first, last),
        out_shape=out_shape,
        in_specs=[SMEM] + [VMEM] * (1 + len(arrays) + (0 if first else 2)),
        out_specs=[VMEM] * len(out_shape),
        scratch_shapes=[pltpu.VMEM((TOK, W), jnp.bfloat16)] if last else [],
        compiler_params=pltpu.CompilerParams(vmem_limit_bytes=32 * 1024 * 1024),
        cost_estimate=LIGHT,
        name="attend" + str(len(names)),
    )(band, q, *arrays, *(() if first else state))


def shards(queries, keys, values, band):
    barrier = lax.optimization_barrier
    *pieces, raw = pack(keys, values, queries)
    z4_raw = move(raw, from_z(4))
    own, q = join(over_heads(pieces))

    xnext, xprev = move(own, from_x(1)), move(own, from_x(-1))
    next1, prev1 = move(own, from_chip(1)), move(own, from_chip(-1))
    own_then, z4_raw = barrier((own, z4_raw))
    z4_packed = unpack(z4_raw)
    z4 = lax.all_to_all(z4_packed, "head", split_axis=0, concat_axis=0, tiled=True)

    def step(state, last=False, **blocks):
        blocks = {k: b if isinstance(b, tuple) else ("joint", b) for k, b in blocks.items()}
        return attend(band, q, blocks, state, last)

    z = (lax.axis_index("frame") // CS) % ZS
    up, down = jnp.where(z < 2, xnext, own), jnp.where(z >= ZS - 2, xprev, own)
    next2, prev2 = move(up, from_z(2)), move(down, from_z(-2))
    sent, *_ = barrier((own_then, next1, prev1, up, down))
    partner = move(sent, FROM_PARTNER)
    z4x = move(z4, FROM_X_FOR_8)
    sent, sent1, sent2, *_ = barrier((own, next1, prev1, z4))
    x2 = move(sent, from_x(2))
    next1p, prev1p = move(sent1, FROM_PARTNER), move(sent2, FROM_PARTNER)
    state = step(
        None, own=own, partner=partner, xnext=xnext, xprev=xprev, z4=z4, next1=next1, prev1=prev1
    )
    next2, prev2, z4x, x2, state = barrier((next2, prev2, z4x, x2, state))
    next2p = move(next2, FROM_PARTNER)
    sent, _ = barrier((prev2, next2p))
    prev2p = move(sent, FROM_PARTNER)
    outs = step(
        state,
        True,
        next1p=next1p,
        prev1p=prev1p,
        x2=x2,
        z4x=z4x,
        next2=next2,
        prev2=prev2,
        far2p=("choice", prev2p, next2p),
    )
    return place(over_heads(outs))


def solution(mesh):
    placed = (
        P(("frame", "head"), None),
        P(("frame", "head"), None),
        P(("frame", "head"), None),
        P("frame", None),
    )
    return jax.shard_map(
        shards, mesh=mesh, in_specs=placed, out_specs=P(("frame", "head"), None), check_vma=False
    )
```

```python
import functools
import math

import jax
import jax.numpy as jnp
from jax import lax
from jax.experimental import pallas as pl
from jax.experimental.pallas import tpu as pltpu
from jax.sharding import PartitionSpec as P

HEAD_DIM = 128
TOK = 256
QUARTER = 64
HEADS_HERE = 3
W = HEADS_HERE * HEAD_DIM
XS, ZS, CS, YS = 4, 8, 2, 4
FRAMES = XS * ZS * CS
SCALE = HEAD_DIM**-0.5 * math.log2(math.e)
VMEM = pl.BlockSpec(memory_space=pltpu.VMEM)
LIGHT = pl.CostEstimate(flops=1, bytes_accessed=1, transcendentals=0)
SMEM = pl.BlockSpec(memory_space=pltpu.SMEM)


def frame_of(x, z, core):
    return ((x % XS) * ZS + z % ZS) * CS + core


def route(source):
    return [
        (frame_of(*source(x, z, c)), frame_of(x, z, c))
        for x in range(XS)
        for z in range(ZS)
        for c in range(CS)
    ]


def from_z(step):
    return route(lambda x, z, c: (x, z + step, c))


def from_x(step):
    return route(lambda x, z, c: (x + step, z, c))


def from_chip(step):
    return [((f + step * CS) % FRAMES, f) for f in range(FRAMES)]


FROM_PARTNER = route(lambda x, z, c: (x, z, 1 - c))
FROM_X_FOR_8 = route(lambda x, z, c: (x - 1 if z < ZS // 2 else x + 1, z, c))


def move(block, pairs):
    return lax.ppermute(block, "frame", pairs)


def copy_all(pairs):
    for source, out in pairs:
        out[...] = source[...]


def copier(kernel, out_shape, name):
    return lambda *arrays: pl.pallas_call(
        kernel,
        out_shape=out_shape,
        in_specs=[VMEM] * len(arrays),
        out_specs=[VMEM] * len(out_shape),
        cost_estimate=LIGHT,
        name=name,
    )(*arrays)


def bf16(rows, columns):
    return jax.ShapeDtypeStruct((rows, columns), jnp.bfloat16)


def group_at(group):
    return pl.ds(pl.multiple_of(group * W, W), W)


def quarter_at(quarter):
    return pl.ds(pl.multiple_of(quarter * QUARTER, QUARTER), QUARTER)


def pack_kernel(k_ref, v_ref, q_ref, p0, p1, p2, p3, raw_ref):
    y = lax.axis_index("head")
    pairs = []
    for step, out in enumerate((p0, p1, p2, p3)):
        for i, ref in enumerate((k_ref, v_ref, q_ref)):
            pairs.append((ref.at[:, group_at((y + step) % YS)], out.at[:, i * W : (i + 1) * W]))
    for i, ref in enumerate((k_ref, v_ref)):
        pairs.append((ref, raw_ref.at[:, i * YS * W : (i + 1) * YS * W]))
    copy_all(pairs)


def pack(keys, values, queries):
    out_shape = [bf16(QUARTER, 3 * W)] * YS + [bf16(QUARTER, 2 * YS * W)]
    return copier(pack_kernel, out_shape, "pack")(keys, values, queries)


def unpack_kernel(raw_ref, out_ref):
    pairs = []
    for g in range(YS):
        for i in range(2):
            at = (i * YS + g) * W
            out = out_ref.at[g * QUARTER : (g + 1) * QUARTER, i * W : (i + 1) * W]
            pairs.append((raw_ref.at[:, at : at + W], out))
    copy_all(pairs)


def unpack(raw):
    return copier(unpack_kernel, [bf16(TOK, 2 * W)], "unpack")(raw)[0]


def join_kernel(p0, p1, p2, p3, kv_ref, q_ref):
    y = lax.axis_index("head")
    pairs = []
    for step, piece in enumerate((p0, p1, p2, p3)):
        rows = quarter_at((y + YS - step) % YS)
        pairs.append((piece.at[:, : 2 * W], kv_ref.at[rows, :]))
        pairs.append((piece.at[:, 2 * W :], q_ref.at[rows, :]))
    copy_all(pairs)


def join(pieces):
    return copier(join_kernel, [bf16(TOK, 2 * W), bf16(TOK, W)], "join")(*pieces)


def place_kernel(p0, p1, p2, p3, out_ref):
    y = lax.axis_index("head")
    pairs = [
        (piece, out_ref.at[:, group_at((y + YS - step) % YS)])
        for step, piece in enumerate((p0, p1, p2, p3))
    ]
    copy_all(pairs)


def place(pieces):
    return copier(place_kernel, [bf16(QUARTER, YS * W)], "place")(*pieces)[0]


def y_from(step):
    return [((y - step) % YS, y) for y in range(YS)]


def over_heads(pieces):
    return [pieces[0]] + [lax.ppermute(pieces[s], "head", y_from(s)) for s in range(1, YS)]


BLOCKS = {
    "own": (lambda f, x, z, c: f, None),
    "partner": (lambda f, x, z, c: f + 1 - 2 * c, 128),
    "next1": (lambda f, x, z, c: f + 2, 64),
    "prev1": (lambda f, x, z, c: f - 2, 64),
    "next1p": (lambda f, x, z, c: f + 3 - 2 * c, 128),
    "prev1p": (lambda f, x, z, c: f - 1 - 2 * c, 128),
    "next2": (lambda f, x, z, c: f + 4, 32),
    "prev2": (lambda f, x, z, c: f - 4, 32),
    "far2p": (lambda f, x, z, c: f - 3 + 6 * c, 64),
    "z4": (lambda f, x, z, c: jnp.where(z < 4, f + 8, f - 8), 32),
    "z4x": (lambda f, x, z, c: jnp.where(z < 4, f - 8, f + 8), 32),
    "xnext": (lambda f, x, z, c: f + 16, 32),
    "xprev": (lambda f, x, z, c: f - 16, 32),
    "x2": (lambda f, x, z, c: jnp.where(x < 2, f + 32, f - 32), 32),
}
ROWS = 128
HALF = 64
FAR_STARTS = (0, 32, 96, 128)


def dot_t(a, b):
    return lax.dot_general(a, b, (((1,), (1,)), ((), ())), preferred_element_type=jnp.float32)


def attend_kernel(names, kinds, first, last, band_ref, q_ref, *refs):
    core = lax.axis_index("frame") % CS
    blocks, at = [], 0
    for kind in kinds:
        blocks.append(refs[at : at + (1 if kind == "joint" else 2)])
        at += len(blocks[-1])
    refs = refs[at:]

    def block(i, rows, columns, value):
        kind, parts = kinds[i], blocks[i]
        if kind == "split":
            return parts[value][rows, columns]
        columns = slice(columns.start + value * W, columns.stop + value * W)
        here = parts[0][rows, columns]
        if kind == "choice":
            here = jnp.where(core == 0, here, parts[1][rows, columns])
        return here

    whole = slice(0, TOK)
    if not first:
        stats_in, acc_in = refs[:2]
        refs = refs[2:]
    f = lax.axis_index("frame")
    x, z = f // (ZS * CS), (f // CS) % ZS
    bands = []
    for name in names:
        frame_at, reach = BLOCKS[name]
        if reach is None:
            bands.append(None)
            continue
        g = frame_at(f, x, z, core)
        inside = (g >= 0) & (g < FRAMES)
        bands.append(jnp.where(inside, band_ref[0, jnp.clip(g, 0, FRAMES - 1)], -1))
    far = [i for i, n in enumerate(names) if BLOCKS[n][1] == 32]
    near = [i for i in range(len(names)) if i not in far]
    gaps = {}
    for part in range(TOK // ROWS):
        row0 = part * ROWS
        gap = lax.broadcasted_iota(jnp.int32, (ROWS, TOK), 0) - lax.broadcasted_iota(
            jnp.int32, (ROWS, TOK), 1
        )
        starts = FAR_STARTS[part * 2 : part * 2 + 2]
        far_gap = lax.broadcasted_iota(jnp.int32, (HALF, ROWS), 0) - lax.broadcasted_iota(
            jnp.int32, (HALF, ROWS), 1
        )
        gaps[part] = (
            jnp.abs(gap + row0),
            jnp.abs(
                jnp.concatenate([far_gap + (row0 + j * HALF - starts[j]) for j in range(2)], axis=0)
            ),
            starts,
        )

    units = [(part, h) for part in range(TOK // ROWS) for h in range(HEADS_HERE)]
    size = len(units) if len(names) <= 2 else HEADS_HERE
    for u0 in range(0, len(units), size):
        group = units[u0 : u0 + size]
        tiles, tops, fades, ps, totals, outs = {}, {}, {}, {}, {}, {}
        for u in group:
            part, h = u
            near_gap, far_gap, starts = gaps[part]
            rows = slice(part * ROWS, (part + 1) * ROWS)
            kc = slice(h * HEAD_DIM, (h + 1) * HEAD_DIM)
            q = q_ref[rows, kc]
            for i in near:
                s = dot_t(q, block(i, whole, kc, 0)) * SCALE
                if bands[i] is not None:
                    s = jnp.where(near_gap <= bands[i], s, -jnp.inf)
                tiles[u, i] = s
            for i in far:
                s = [
                    dot_t(
                        q[j * HALF : (j + 1) * HALF],
                        block(i, slice(starts[j], starts[j] + ROWS), kc, 0),
                    )
                    for j in range(2)
                ]
                s = jnp.concatenate(s, axis=0) * SCALE
                tiles[u, i] = jnp.where(far_gap <= bands[i], s, -jnp.inf)
        for u in group:
            parts = [
                tiles[u, i][:, c0 : c0 + 128]
                for i in range(len(names))
                for c0 in range(0, tiles[u, i].shape[1], 128)
            ]
            tops[u] = jnp.max(functools.reduce(jnp.maximum, parts), axis=1, keepdims=True)
        if not first:
            for u in group:
                part, h = u
                rows = slice(part * ROWS, (part + 1) * ROWS)
                top_in = stats_in[rows, h : h + 1]
                tops[u] = jnp.maximum(tops[u], top_in)
                fades[u] = jnp.exp2(top_in - tops[u])
        for u in group:
            parts = []
            for i in range(len(names)):
                p = jnp.exp2(tiles[u, i] - tops[u])
                parts += [p[:, c0 : c0 + 128] for c0 in range(0, p.shape[1], 128)]
                ps[u, i] = p.astype(jnp.bfloat16)
            totals[u] = jnp.sum(functools.reduce(jnp.add, parts), axis=1, keepdims=True)
        for u in group:
            part, h = u
            starts = gaps[part][2]
            kc = slice(h * HEAD_DIM, (h + 1) * HEAD_DIM)
            parts = []
            for i in range(len(names)):
                p = ps[u, i]
                if i in near:
                    o = jnp.dot(p, block(i, whole, kc, 1), preferred_element_type=jnp.float32)
                else:
                    o = [
                        jnp.dot(
                            p[j * HALF : (j + 1) * HALF],
                            block(i, slice(starts[j], starts[j] + ROWS), kc, 1),
                            preferred_element_type=jnp.float32,
                        )
                        for j in range(2)
                    ]
                    o = jnp.concatenate(o, axis=0)
                parts.append(o)
            outs[u] = functools.reduce(jnp.add, parts)
        for u in group:
            part, h = u
            rows = slice(part * ROWS, (part + 1) * ROWS)
            kc = slice(h * HEAD_DIM, (h + 1) * HEAD_DIM)
            total, out = totals[u], outs[u]
            if not first:
                total = total + stats_in[rows, 4 + h : 5 + h] * fades[u]
                out = out + acc_in[rows, kc] * fades[u]
            if last:
                refs[YS][rows, kc] = (out * (1.0 / total)).astype(jnp.bfloat16)
            else:
                refs[0][rows, h : h + 1] = tops[u]
                refs[0][rows, 4 + h : 5 + h] = total
                refs[1][rows, kc] = out
    if last:
        y = lax.axis_index("head")
        for step in range(YS):
            rows = pl.ds(pl.multiple_of(((y + step) % YS) * QUARTER, QUARTER), QUARTER)
            refs[step][...] = refs[YS][rows, :]


def attend(band, q, blocks, state, last):
    names = list(blocks)
    first = state is None
    kinds, arrays = [], []
    for block in blocks.values():
        kinds.append(block[0])
        arrays += block[1:]
    if last:
        out_shape = [jax.ShapeDtypeStruct((QUARTER, W), jnp.bfloat16)] * YS
    else:
        out_shape = [
            jax.ShapeDtypeStruct((TOK, 128), jnp.float32),
            jax.ShapeDtypeStruct((TOK, W), jnp.float32),
        ]
    return pl.pallas_call(
        functools.partial(attend_kernel, names, kinds, first, last),
        out_shape=out_shape,
        in_specs=[SMEM] + [VMEM] * (1 + len(arrays) + (0 if first else 2)),
        out_specs=[VMEM] * len(out_shape),
        scratch_shapes=[pltpu.VMEM((TOK, W), jnp.bfloat16)] if last else [],
        compiler_params=pltpu.CompilerParams(vmem_limit_bytes=32 * 1024 * 1024),
        cost_estimate=LIGHT,
        name="attend" + str(len(names)),
    )(band, q, *arrays, *(() if first else state))


def shards(queries, keys, values, band):
    barrier = lax.optimization_barrier
    *pieces, raw = pack(keys, values, queries)
    z4_raw = move(raw, from_z(4))
    own, q = join(over_heads(pieces))

    xnext, xprev = move(own, from_x(1)), move(own, from_x(-1))
    next1, prev1 = move(own, from_chip(1)), move(own, from_chip(-1))
    sent, z4_raw = barrier((own, z4_raw))
    partner = move(sent, FROM_PARTNER)
    z4_packed = unpack(z4_raw)
    z4 = lax.all_to_all(z4_packed, "head", split_axis=0, concat_axis=0, tiled=True)

    def step(state, last=False, **blocks):
        blocks = {k: b if isinstance(b, tuple) else ("joint", b) for k, b in blocks.items()}
        return attend(band, q, blocks, state, last)

    z = (lax.axis_index("frame") // CS) % ZS
    next2 = move(jnp.where(z < 2, xnext, own), from_z(2))
    prev2 = move(jnp.where(z >= ZS - 2, xprev, own), from_z(-2))
    z4x = move(z4, FROM_X_FOR_8)
    sent, sent1, sent2, *_ = barrier((own, next1, prev1, z4_packed))
    x2 = move(sent, from_x(2))
    next1p, prev1p = move(sent1, FROM_PARTNER), move(sent2, FROM_PARTNER)
    state = step(None, own=own, xnext=xnext, xprev=xprev, z4=z4, next1=next1, prev1=prev1)
    next2, prev2, z4x, x2, state = barrier((next2, prev2, z4x, x2, state))
    next2p = move(next2, FROM_PARTNER)
    sent, _ = barrier((prev2, next2p))
    prev2p = move(sent, FROM_PARTNER)
    outs = step(
        state,
        True,
        partner=partner,
        next1p=next1p,
        prev1p=prev1p,
        x2=x2,
        z4x=z4x,
        next2=next2,
        prev2=prev2,
        far2p=("choice", prev2p, next2p),
    )
    return place(over_heads(outs))


def solution(mesh):
    placed = (
        P(("frame", "head"), None),
        P(("frame", "head"), None),
        P(("frame", "head"), None),
        P("frame", None),
    )
    return jax.shard_map(
        shards, mesh=mesh, in_specs=placed, out_specs=P(("frame", "head"), None), check_vma=False
    )
```
